128 devices in a mesh: head: 4 (over y), ctx: 32 (over x, z, core).
Axes of the slice: x: 4, y: 4, z: 4, core: 2. Of those that a mesh axis runs over, the one named last changes fastest.
Arguments:
- queries: bfloat16 [32, 512, 8192], P('ctx', 'head'), may hold values from -6 to 6
- keys: bfloat16 [32, 512, 8192], P('ctx', 'head'), may hold values from -6 to 6
- values: bfloat16 [32, 512, 8192], P('ctx', 'head'), may hold values from -6 to 6
- gate: bfloat16 [32, 512, 8192], P('ctx', 'head'), may hold values from -6 to 6
- log_decay: float32 [32, 64, 512], P('ctx', 'head'), may hold values from -1 to 0, as said below
- norm_gain: bfloat16 [8192], P('head'), may hold values from 0.099609375 to 1.8984375
Outputs:
- attended: bfloat16 [32, 512, 8192], P('ctx', 'head')
The draws below stay inside these ranges and needn't reach their ends.
Inputs may be any that keep to these rules, and one draw needn't show every extreme that they name: `log_decay`: every entry is negative.
All inputs are finite; a program needn't handle non-finite values.
Results may differ from the reference program's by a relative error of at most 0.0048.
Values may be sent and summed in bfloat16 or wider, within the bound.
A program may use at most 192 MiB of HBM per device.

```python
import math
import jax
import jax.numpy as jnp
from jax import lax

HEAD_COUNT = 64
DH = 128
HD = 8192
BLOCK_GROUPS = 32
BLOCK_LENGTH = 512
SEQUENCE_TOKENS = 16384


def draw_log_decay(key, part):
    key = jax.random.fold_in(key, 7)
    token_flows = jax.random.split(key, 5)
    fast_share = 0.5
    fast_heads = jax.random.uniform(token_flows[0], (HEAD_COUNT,)) < fast_share
    slow_rate = math.log(2.0) / (2.0 * SEQUENCE_TOKENS)
    base_rate = jnp.where(fast_heads, 1.0 / 40.0, slow_rate)
    block_factor = jnp.exp(jax.random.uniform(token_flows[1], (BLOCK_GROUPS, HEAD_COUNT, 1), minval=math.log(0.5), maxval=math.log(2.0)))
    roughness = jax.random.uniform(token_flows[2], (BLOCK_GROUPS, HEAD_COUNT, BLOCK_LENGTH), minval=0.5, maxval=1.5)
    decay_rate = base_rate[None, :, None] * block_factor * roughness
    block_runs = jax.random.uniform(token_flows[3], (BLOCK_GROUPS, HEAD_COUNT, BLOCK_LENGTH)) < 2.0 / SEQUENCE_TOKENS
    retained_fraction = jax.random.uniform(token_flows[4], (BLOCK_GROUPS, HEAD_COUNT, BLOCK_LENGTH), minval=0.5, maxval=0.8)
    return (jnp.where(block_runs, jnp.log(retained_fraction), 0.0) - decay_rate).astype(jnp.float32)


def levels(stream_key, dims, cuts, least, largest):
    gain = 1.0
    for dim, shards_of in cuts:
        steps = jax.random.uniform(jax.random.fold_in(jax.random.fold_in(stream_key, 6), dim), (shards_of,), jnp.float32, least / len(cuts), largest / len(cuts))
        gain = gain * jnp.repeat(jnp.exp(steps), dims[dim] // shards_of).reshape((-1,) + (1,) * (len(dims) - 1 - dim))
    return gain


def gaussian(own_key, dims, width, limit, pieces=(), held_as=jnp.bfloat16):
    result = jax.random.normal(own_key, dims, jnp.float32) * width
    if len(pieces) > 0:
        result = levels(own_key, dims, pieces, -0.22, 0.18) * result
    return jnp.clip(result, min=-limit, max=limit).astype(held_as)


def setup_inputs(seed: int = 0) -> dict:
    key_of = jax.random.split(jax.random.key(seed), 7)
    queries = gaussian(key_of[0], (BLOCK_GROUPS, BLOCK_LENGTH, HD), 1.0, 6.0, ((0, 32), (1, 4)))
    keys = gaussian(key_of[1], (BLOCK_GROUPS, BLOCK_LENGTH, HD), 1.0, 6.0, ((0, 32), (1, 4)))
    values = gaussian(key_of[2], (BLOCK_GROUPS, BLOCK_LENGTH, HD), 1.0, 6.0, ((0, 32), (1, 4)))
    gate = gaussian(key_of[3], (BLOCK_GROUPS, BLOCK_LENGTH, HD), 1.5, 6.0, ((0, 32), (1, 4)))
    log_decay = draw_log_decay(jax.random.fold_in(key_of[6], 71), 0)
    norm_gain = jnp.clip(1.0 + 0.18 * jax.random.normal(key_of[5], (HD,), jnp.float32), 0.099609375, 1.8984375).astype(jnp.bfloat16)
    return dict(queries=queries, keys=keys, values=values, gate=gate, log_decay=log_decay, norm_gain=norm_gain)


def reference(queries, keys, values, gate, log_decay, norm_gain):
    position = jnp.arange(BLOCK_LENGTH)
    causal_mask = position[:, None] >= position[None, :]
    gain_wide = norm_gain.astype(jnp.float32)

    def group_step(carry_state, inputs):
        query_group, key_group, value_group, gate_group, decay_group = inputs
        query_heads = query_group.reshape(BLOCK_LENGTH, HEAD_COUNT, DH).astype(jnp.float32)
        key_heads = key_group.reshape(BLOCK_LENGTH, HEAD_COUNT, DH).astype(jnp.float32)
        value_heads = value_group.reshape(BLOCK_LENGTH, HEAD_COUNT, DH).astype(jnp.float32)
        cumulative = jnp.cumsum(decay_group, axis=-1)
        group_total = cumulative[:, -1]
        scores = jnp.einsum('thd,shd->hts', query_heads, key_heads)
        log_gap = cumulative[:, :, None] - cumulative[:, None, :]
        weights = (scores * jnp.exp(jnp.where(causal_mask[None], log_gap, -jnp.inf))).astype(jnp.bfloat16)
        inside_part = jnp.einsum('hts,shd->thd', weights.astype(jnp.float32), value_heads)
        carried_part = jnp.einsum('thd,hde->the', query_heads, carry_state, precision=lax.Precision.HIGHEST)
        mixed = inside_part + carried_part * jnp.exp(cumulative).T[:, :, None]
        inv_rms = lax.rsqrt(lax.optimization_barrier(jnp.mean(mixed * mixed, axis=-1, keepdims=True)) + 1e-06)
        normed = (mixed * inv_rms).reshape(BLOCK_LENGTH, HEAD_COUNT * DH) * gain_wide * jax.nn.sigmoid(gate_group.astype(jnp.float32))
        decayed_keys = (key_heads * jnp.exp(group_total[None, :] - cumulative.T)[:, :, None]).astype(jnp.bfloat16)
        block_state = jnp.einsum('thd,the->hde', decayed_keys.astype(jnp.float32), value_heads)
        next_state = jnp.exp(group_total)[:, None, None] * carry_state + block_state
        return (next_state, normed.astype(jnp.bfloat16))
    empty_state = jnp.zeros((HEAD_COUNT, DH, DH), jnp.float32)
    _, outputs = lax.scan(group_step, empty_state, (queries, keys, values, gate, log_decay))
    return outputs
```

```python
import functools

import jax
import jax.numpy as jnp
from jax import lax
from jax.experimental import pallas as pl
from jax.experimental.pallas import tpu as pltpu
from jax.sharding import PartitionSpec as P

MESH = pl.DeviceIdType.MESH
F32 = jnp.float32
BF16 = jnp.bfloat16
DH = 128
PAD = 8
HIGHEST = lax.Precision.HIGHEST


def at_lanes(head):
    return pl.ds(pl.multiple_of(head * DH, DH), DH)


def kernel(
    dims,
    q_hbm, k_hbm, v_hbm, g_hbm, ld_hbm, gain_hbm,
    o_hbm,
    q, k, v, g, o,
    ld, gain_in, gain,
    cum_row, dec_row, cum_col, step_decay, block_decay,
    s_out, s_in, b_out, b_in, t_out, t_in, c_now, c_out, c_in, p_out, p_in,
    inside, gated,
    load_sem, store_sem,
    ld_send, ld_recv, gain_send, gain_recv,
    s_send, s_recv, b_send, b_recv, t_send, t_recv, c_send, c_recv, p_send, p_recv,
):
    ny, nx, nzc, halves = dims
    rows = q.shape[0]
    per_owner = halves * nzc
    heads = ny * per_owner
    y = lax.axis_index("head")
    ctx = lax.axis_index("ctx")
    x = ctx // nzc
    zc = ctx % nzc

    def load(n, src, dst):
        return pltpu.make_async_copy(src, dst, load_sem.at[n])

    loads = [
        load(0, ld_hbm, ld.at[y]),
        load(1, gain_hbm, gain_in.at[y]),
        load(2, k_hbm, k),
        load(3, v_hbm, v),
        load(4, q_hbm, q),
        load(5, g_hbm, g),
    ]
    for one in loads:
        one.start()

    barrier = pltpu.get_barrier_semaphore()
    peers = [{"head": lax.rem(y + d, ny)} for d in range(1, ny)]
    peers += [{"ctx": x * nzc + lax.rem(zc + e, nzc)} for e in range(1, nzc)]
    peers += [{"ctx": lax.rem(x + d, nx) * nzc + zc} for d in range(1, nx)]
    for peer in peers:
        pl.semaphore_signal(barrier, inc=1, device_id=peer, device_id_type=MESH)
    pl.semaphore_wait(barrier, len(peers))

    def remote(src, dst, send, recv, peer):
        return pltpu.make_async_remote_copy(
            src_ref=src, dst_ref=dst, send_sem=send, recv_sem=recv,
            device_id=peer, device_id_type=MESH,
        )

    def ld_copy(d, source):
        peer = {"head": lax.rem(y + d, ny)}
        return remote(ld.at[source], ld.at[source], ld_send.at[d - 1], ld_recv.at[d - 1], peer)

    def gain_copy(d, source):
        peer = {"head": lax.rem(y + d, ny)}
        return remote(
            gain_in.at[source], gain_in.at[source], gain_send.at[d - 1], gain_recv.at[d - 1], peer
        )

    loads[0].wait()
    for d in range(1, ny):
        ld_copy(d, y).start()
    loads[1].wait()
    for d in range(1, ny):
        gain_copy(d, y).start()
    for d in range(1, ny):
        ld_copy(d, lax.rem(y + ny - d, ny)).wait_recv()

    upper = (
        lax.broadcasted_iota(jnp.int32, (rows, rows), 0)
        <= lax.broadcasted_iota(jnp.int32, (rows, rows), 1)
    ).astype(F32)
    mine = pl.ds(pl.multiple_of(y * rows, rows), rows)
    cum_col[...] = jnp.zeros_like(cum_col)
    for group in range(ny):
        cumulative = jnp.dot(
            ld[group, :, mine], upper, precision=HIGHEST, preferred_element_type=F32
        )
        here = pl.ds(group * per_owner, per_owner)
        cum_row[here, :] = cumulative
        dec_row[here, :] = jnp.exp(cumulative[:, rows - 1 :] - cumulative)
        cum_col[here, :] = cumulative
    cum_col[...] = cum_col[...].T
    whole = jnp.zeros((per_owner, 1), F32)
    for part in range(ny):
        total = jnp.sum(ld[y, :, part * rows : (part + 1) * rows], axis=1, keepdims=True)
        step_decay[part] = jnp.broadcast_to(jnp.exp(total), (per_owner, DH))
        whole = whole + total
    block_decay[...] = jnp.broadcast_to(jnp.exp(whole), (per_owner, DH))

    def s_copy(half, d, source, peer_group):
        here = pl.ds(peer_group * per_owner + half * nzc, nzc)
        there = pl.ds(half * nzc, nzc)
        return remote(
            s_out.at[here], s_in.at[source, there], s_send.at[half, d - 1], s_recv.at[half, d - 1],
            {"head": lax.rem(y + d, ny)},
        )

    def state_of(head):
        lanes = at_lanes(head)
        decayed = (k[:, lanes].astype(F32).T * dec_row[pl.ds(head, 1), :]).astype(BF16)
        return jnp.dot(decayed, v[:, lanes], preferred_element_type=F32).astype(BF16)

    order = [d for d in (2, 1, 3) if d < ny]
    loads[2].wait()
    loads[3].wait()
    for half in range(halves):
        for d in order + [0]:
            group = lax.rem(y + d, ny)

            def one_state(j, _, group=group, half=half, d=d):
                local = half * nzc + j
                state = state_of(group * per_owner + local)
                if d == 0:
                    s_in[y, local] = state
                else:
                    s_out[group * per_owner + local] = state
                return 0

            lax.fori_loop(0, nzc, one_state, 0)
            if d:
                s_copy(half, d, y, group).start()

    loads[4].wait()
    loads[5].wait()
    for d in range(1, ny):
        gain_copy(d, lax.rem(y + ny - d, ny)).wait_recv()
    for group in range(ny):
        gain[pl.ds(group * per_owner, per_owner), :] = gain_in[group].astype(F32)

    causal = lax.broadcasted_iota(jnp.int32, (rows, rows), 0) >= lax.broadcasted_iota(
        jnp.int32, (rows, rows), 1
    )

    def column_of(head):
        turned = pltpu.roll(cum_col[...], lax.rem(DH - head, DH), axis=1)
        return jnp.broadcast_to(turned[:, :1], (rows, rows))

    def one_inside(head, _):
        lanes = at_lanes(head)
        scores = lax.dot_general(
            q[:, lanes], k[:, lanes], (((1,), (1,)), ((), ())), preferred_element_type=F32
        )
        gap = jnp.where(causal, column_of(head) - cum_row[pl.ds(head, 1), :], -jnp.inf)
        weights = (scores * jnp.exp(gap)).astype(BF16)
        inside[:, lanes] = jnp.dot(weights, v[:, lanes], preferred_element_type=F32)
        gated[:, lanes] = jax.nn.sigmoid(g[:, lanes].astype(F32)) * gain[pl.ds(head, 1), :]
        return 0

    def b_copy(half, e, source, owner):
        return remote(
            b_out.at[half, owner], b_in.at[half, source], b_send.at[half, e - 1],
            b_recv.at[half, e - 1], {"ctx": x * nzc + owner},
        )

    def t_copy(half, d):
        return remote(
            t_out.at[half], t_in.at[half, d - 1], t_send.at[half, d - 1], t_recv.at[half, d - 1],
            {"ctx": lax.rem(x + d, nx) * nzc + zc},
        )

    def c_copy(half, e, source, block):
        return remote(
            c_out.at[half, block], c_in.at[half, source], c_send.at[half, e - 1],
            c_recv.at[half, e - 1], {"ctx": x * nzc + block},
        )

    def p_copy(half, d, source, part):
        there = pl.ds(half * nzc, nzc)
        return remote(
            p_out.at[part, there], p_in.at[source, there], p_send.at[half, d - 1],
            p_recv.at[half, d - 1], {"head": part},
        )

    def make_totals(half):
        for d in range(1, ny):
            s_copy(half, d, lax.rem(y + ny - d, ny), lax.rem(y + d, ny)).wait_recv()

        def one_total(r, _):
            local = half * nzc + r
            total = s_in[0, local].astype(F32)
            for part in range(1, ny):
                total = total * step_decay[part, pl.ds(local, 1), :] + s_in[part, local].astype(F32)
            b_out[half, r, :DH, :] = total
            b_out[half, r, DH:, :] = jnp.broadcast_to(block_decay[pl.ds(local, 1), :], (PAD, DH))
            return 0

        lax.fori_loop(0, nzc, one_total, 0)
        for e in range(1, nzc):
            b_copy(half, e, zc, lax.rem(zc + e, nzc)).start()
        b_in[half, zc] = b_out[half, zc]

    def make_group_total(half):
        for e in range(1, nzc):
            b_copy(half, e, lax.rem(zc + nzc - e, nzc), lax.rem(zc + e, nzc)).wait_recv()
        total = b_in[half, 0, :DH, :]
        decay = b_in[half, 0, DH:, :]
        for block in range(1, nzc):
            step = b_in[half, block, DH:, :]
            total = total * step[:1] + b_in[half, block, :DH, :]
            decay = decay * step
        t_out[half, :DH, :] = total
        t_out[half, DH:, :] = decay
        for d in range(1, nx):

            @pl.when(x + d < nx)
            def _(d=d):
                t_copy(half, d).start()

    def make_carried(half):
        c_now[...] = jnp.zeros_like(c_now)
        for d in range(nx - 1, 0, -1):

            @pl.when(x >= d)
            def _(d=d):
                t_copy(half, d).wait_recv()
                c_now[...] = c_now[...] * t_in[half, d - 1, DH : DH + 1, :] + t_in[half, d - 1, :DH, :]

        state = c_now[...]
        for block in range(nzc):
            c_out[half, block] = state
            if block + 1 < nzc:
                state = state * b_in[half, block, DH : DH + 1, :] + b_in[half, block, :DH, :]
        for e in range(1, nzc):
            c_copy(half, e, zc, lax.rem(zc + e, nzc)).start()
        c_in[half, zc] = c_out[half, zc]

    def make_prefixes(half):
        for e in range(1, nzc):
            c_copy(half, e, lax.rem(zc + nzc - e, nzc), lax.rem(zc + e, nzc)).wait_recv()

        def one_prefix(r, _):
            local = half * nzc + r
            state = c_in[half, r]
            for part in range(ny):
                p_out[part, local] = state.astype(BF16)
                if part + 1 < ny:
                    decay = step_decay[part, pl.ds(local, 1), :]
                    state = state * decay + s_in[part, local].astype(F32)
            return 0

        lax.fori_loop(0, nzc, one_prefix, 0)
        for d in order:
            p_copy(half, d, y, lax.rem(y + d, ny)).start()
        there = pl.ds(half * nzc, nzc)
        p_in[y, there] = p_out[y, there]

    def store(half, group, d):
        lanes = pl.ds(pl.multiple_of((group * per_owner + half * nzc) * DH, DH), nzc * DH)
        return pltpu.make_async_copy(o.at[:, lanes], o_hbm.at[:, lanes], store_sem.at[half, d])

    def make_outputs(half, d):
        group = lax.rem(y + ny - d, ny)
        if d:
            p_copy(half, d, group, lax.rem(y + d, ny)).wait_recv()

        def one_output(j, _):
            local = half * nzc + j
            head = group * per_owner + local
            lanes = at_lanes(head)
            from_state = jnp.dot(q[:, lanes], p_in[group, local], preferred_element_type=F32)
            mixed = inside[:, lanes] + jnp.exp(column_of(head)) * from_state
            scale = lax.rsqrt(jnp.mean(mixed * mixed, axis=1, keepdims=True) + 1e-6)
            o[:, lanes] = (mixed * scale * gated[:, lanes]).astype(BF16)
            return 0

        lax.fori_loop(0, nzc, one_output, 0)
        store(half, group, d).start()

    quarter = heads // 4
    lax.fori_loop(0, quarter, one_inside, 0)
    make_totals(0)
    lax.fori_loop(quarter, 2 * quarter, one_inside, 0)
    make_group_total(0)
    lax.fori_loop(2 * quarter, 3 * quarter, one_inside, 0)
    make_carried(0)
    make_totals(1)
    lax.fori_loop(3 * quarter, heads, one_inside, 0)
    make_prefixes(0)
    make_group_total(1)
    make_outputs(0, 0)
    make_carried(1)
    for d in order[:1]:
        make_outputs(0, d)
    make_prefixes(1)
    for d in order[1:]:
        make_outputs(0, d)
    make_outputs(1, 0)
    for d in order:
        make_outputs(1, d)

    for d in range(1, ny):
        ld_copy(d, y).wait_send()
        gain_copy(d, y).wait_send()
    for half in range(halves):
        for d in range(1, ny):
            s_copy(half, d, y, lax.rem(y + d, ny)).wait_send()
            p_copy(half, d, y, lax.rem(y + d, ny)).wait_send()
        for e in range(1, nzc):
            b_copy(half, e, zc, lax.rem(zc + e, nzc)).wait_send()
            c_copy(half, e, zc, lax.rem(zc + e, nzc)).wait_send()
        for d in range(1, nx):

            @pl.when(x + d < nx)
            def _(half=half, d=d):
                t_copy(half, d).wait_send()

        for d in range(ny):
            store(half, lax.rem(y + ny - d, ny), d).wait()


def on_device(dims, queries, keys, values, gate, log_decay, norm_gain):
    ny, nx, nzc, halves = dims
    per_owner = halves * nzc
    heads = ny * per_owner
    _, rows, width = queries.shape
    block = log_decay.shape[2]
    dma = pltpu.SemaphoreType.DMA
    vmem = pltpu.VMEM
    stream = [vmem((rows, width), BF16)] * 5
    out = pl.pallas_call(
        functools.partial(kernel, dims),
        out_shape=jax.ShapeDtypeStruct((rows, width), BF16),
        in_specs=[pl.BlockSpec(memory_space=pl.ANY)] * 6,
        out_specs=pl.BlockSpec(memory_space=pl.ANY),
        scratch_shapes=stream
        + [
            vmem((ny, per_owner, block), F32),
            vmem((ny, per_owner, DH), BF16),
            vmem((heads, DH), F32),
            vmem((heads, rows), F32),
            vmem((heads, rows), F32),
            vmem((rows, rows), F32),
            vmem((ny, per_owner, DH), F32),
            vmem((per_owner, DH), F32),
            vmem((heads, DH, DH), BF16),
            vmem((ny, per_owner, DH, DH), BF16),
            vmem((halves, nzc, DH + PAD, DH), F32),
            vmem((halves, nzc, DH + PAD, DH), F32),
            vmem((halves, DH + PAD, DH), F32),
            vmem((halves, nx - 1, DH + PAD, DH), F32),
            vmem((DH, DH), F32),
            vmem((halves, nzc, DH, DH), F32),
            vmem((halves, nzc, DH, DH), F32),
            vmem((ny, per_owner, DH, DH), BF16),
            vmem((ny, per_owner, DH, DH), BF16),
            vmem((rows, width), F32),
            vmem((rows, width), F32),
            dma((6,)),
            dma((halves, ny)),
            dma((ny - 1,)),
            dma((ny - 1,)),
            dma((ny - 1,)),
            dma((ny - 1,)),
            dma((halves, ny - 1)),
            dma((halves, ny - 1)),
            dma((halves, nzc - 1)),
            dma((halves, nzc - 1)),
            dma((halves, nx - 1)),
            dma((halves, nx - 1)),
            dma((halves, nzc - 1)),
            dma((halves, nzc - 1)),
            dma((halves, ny - 1)),
            dma((halves, ny - 1)),
        ],
        compiler_params=pltpu.CompilerParams(
            collective_id=0, has_side_effects=True, vmem_limit_bytes=52 * 2**20
        ),
        cost_estimate=pl.CostEstimate(
            flops=8 * rows * DH * width, bytes_accessed=10 * rows * width, transcendentals=0
        ),
    )(
        queries[0],
        keys[0],
        values[0],
        gate[0],
        log_decay[0],
        norm_gain.reshape(per_owner, DH),
    )
    return out[None]


def solution(mesh):
    ny = mesh.shape["head"]
    nctx = mesh.shape["ctx"]
    nx = 4 if nctx >= 16 else 2
    halves = 2

    def whole(queries, keys, values, gate, log_decay, norm_gain):
        dims = (ny, nx, nctx // nx, halves)
        return jax.shard_map(
            functools.partial(on_device, dims),
            mesh=mesh,
            in_specs=(P("ctx", "head", None),) * 5 + (P("head"),),
            out_specs=P("ctx", "head", None),
            check_vma=False,
        )(queries, keys, values, gate, log_decay, norm_gain)

    return whole
```

```python
import functools

import jax
import jax.numpy as jnp
from jax import lax
from jax.experimental import pallas as pl
from jax.experimental.pallas import tpu as pltpu
from jax.sharding import PartitionSpec as P

MESH = pl.DeviceIdType.MESH
F32 = jnp.float32
BF16 = jnp.bfloat16
DH = 128
PAD = 8
HIGHEST = lax.Precision.HIGHEST


def kernel(
    dims,
    q_hbm, k_hbm, v_hbm, g_hbm, ld_hbm, gain_hbm,
    o_hbm,
    q, k, v, g, o,
    ld, gain_in, gain,
    cum_row, dec_row, cum_col, exp_col, step_decay, block_decay,
    s_out, s_in, b_out, b_in, t_out, t_in, c_now, c_out, c_in, p_out, p_in,
    inside, gated,
    load_sem, store_sem,
    ld_send, ld_recv, gain_send, gain_recv,
    s_send, s_recv, b_send, b_recv, t_send, t_recv, c_send, c_recv, p_send, p_recv,
):
    ny, nx, nzc, chunks, few = dims
    rows = q.shape[0]
    per_owner = chunks * few
    heads = ny * per_owner
    pieces = nzc // few
    piece = DH // pieces
    y = lax.axis_index("head")
    ctx = lax.axis_index("ctx")
    x = ctx // nzc
    zc = ctx % nzc

    def load(n, src, dst):
        return pltpu.make_async_copy(src, dst, load_sem.at[n])

    loads = [
        load(0, ld_hbm, ld.at[y]),
        load(1, gain_hbm, gain_in.at[y]),
        load(2, k_hbm, k),
        load(3, v_hbm, v),
        load(4, q_hbm, q),
        load(5, g_hbm, g),
    ]
    for one in loads:
        one.start()

    barrier = pltpu.get_barrier_semaphore()
    peers = [{"head": lax.rem(y + d, ny)} for d in range(1, ny)]
    peers += [{"ctx": x * nzc + lax.rem(zc + e, nzc)} for e in range(1, nzc)]
    peers += [{"ctx": lax.rem(x + d, nx) * nzc + zc} for d in range(1, nx)]
    for peer in peers:
        pl.semaphore_signal(barrier, inc=1, device_id=peer, device_id_type=MESH)
    pl.semaphore_wait(barrier, len(peers))

    def remote(src, dst, send, recv, peer):
        return pltpu.make_async_remote_copy(
            src_ref=src, dst_ref=dst, send_sem=send, recv_sem=recv,
            device_id=peer, device_id_type=MESH,
        )

    def ld_copy(d, source):
        peer = {"head": lax.rem(y + d, ny)}
        return remote(ld.at[source], ld.at[source], ld_send.at[d - 1], ld_recv.at[d - 1], peer)

    def gain_copy(d, source):
        peer = {"head": lax.rem(y + d, ny)}
        return remote(
            gain_in.at[source], gain_in.at[source], gain_send.at[d - 1], gain_recv.at[d - 1], peer
        )

    loads[0].wait()
    for d in range(1, ny):
        ld_copy(d, y).start()
    loads[1].wait()
    for d in range(1, ny):
        gain_copy(d, y).start()
    for d in range(1, ny):
        ld_copy(d, lax.rem(y + ny - d, ny)).wait_recv()

    upper = (
        lax.broadcasted_iota(jnp.int32, (rows, rows), 0)
        <= lax.broadcasted_iota(jnp.int32, (rows, rows), 1)
    ).astype(F32)
    mine = pl.ds(pl.multiple_of(y * rows, rows), rows)
    cum_col[...] = jnp.zeros_like(cum_col)
    for group in range(ny):
        cumulative = jnp.dot(
            ld[group, :, mine], upper, precision=HIGHEST, preferred_element_type=F32
        )
        here = pl.ds(group * per_owner, per_owner)
        cum_row[here, :] = cumulative
        dec_row[here, :] = jnp.exp(cumulative[:, rows - 1 :] - cumulative)
        cum_col[here, :] = cumulative
    cum_col[...] = cum_col[...].T
    exp_col[...] = jnp.exp(cum_col[...])
    whole = jnp.zeros((per_owner, 1), F32)
    for part in range(ny):
        total = jnp.sum(ld[y, :, part * rows : (part + 1) * rows], axis=1, keepdims=True)
        step_decay[part] = jnp.broadcast_to(jnp.exp(total), (per_owner, DH))
        whole = whole + total
    block_decay[...] = jnp.broadcast_to(jnp.exp(whole), (per_owner, DH))

    def s_copy(i, d, source, group):
        here = pl.ds(group * per_owner + i * few, few)
        there = pl.ds(i * few, few)
        return remote(
            s_out.at[here], s_in.at[source, there], s_send.at[i, d - 1], s_recv.at[i, d - 1],
            {"head": lax.rem(y + d, ny)},
        )

    def b_copy(i, e, source, owner):
        return remote(
            b_out.at[i, owner], b_in.at[i, source], b_send.at[i, e - 1], b_recv.at[i, e - 1],
            {"ctx": x * nzc + owner},
        )

    def t_copy(i, d):
        return remote(
            t_out.at[i], t_in.at[i, d - 1], t_send.at[i, d - 1], t_recv.at[i, d - 1],
            {"ctx": lax.rem(x + d, nx) * nzc + zc},
        )

    def c_copy(i, e, source, block):
        return remote(
            c_out.at[i, block], c_in.at[i, source], c_send.at[i, e - 1], c_recv.at[i, e - 1],
            {"ctx": x * nzc + block},
        )

    def p_copy(i, d, source, part):
        there = pl.ds(i * few, few)
        return remote(
            p_out.at[part, there], p_in.at[source, there], p_send.at[i, d - 1], p_recv.at[i, d - 1],
            {"head": part},
        )

    def store(i, d):
        group = lax.rem(y + ny - d, ny)
        lanes = pl.ds(pl.multiple_of((group * per_owner + i * few) * DH, DH), few * DH)
        return pltpu.make_async_copy(o.at[:, lanes], o_hbm.at[:, lanes], store_sem.at[i, d])

    def lanes_of(first, j):
        return pl.ds(pl.multiple_of((first + j) * DH, DH), DH)

    far_first = [d for d in (2, 1, 3) if d < ny]

    def make_states(i):
        for d in far_first + [0]:
            group = lax.rem(y + d, ny)
            begin = pl.multiple_of(group * per_owner, per_owner)
            for j in range(i * few, (i + 1) * few):
                lanes = lanes_of(begin, j)
                decay = dec_row[pl.ds(begin, per_owner), :][j : j + 1]
                decayed = (k[:, lanes].T.astype(F32) * decay).astype(BF16)
                state = jnp.dot(decayed, v[:, lanes], preferred_element_type=F32).astype(BF16)
                if d:
                    s_out[begin + j] = state
                else:
                    s_in[y, j] = state

    def send_states(i):
        for d in far_first:
            s_copy(i, d, y, lax.rem(y + d, ny)).start()

    causal = lax.broadcasted_iota(jnp.int32, (rows, rows), 0) >= lax.broadcasted_iota(
        jnp.int32, (rows, rows), 1
    )
    wide = 8 if heads % 8 == 0 else heads

    def make_inside(step):
        first = pl.multiple_of(step * wide, wide)
        columns = pltpu.roll(cum_col[...], lax.rem(DH - first, DH), axis=1)[:, :wide]
        sums = cum_row[pl.ds(first, wide), :]
        gains = gain[pl.ds(first, wide), :]
        for j in range(wide):
            lanes = lanes_of(first, j)
            scores = lax.dot_general(
                q[:, lanes], k[:, lanes], (((1,), (1,)), ((), ())), preferred_element_type=F32
            )
            gap = jnp.where(causal, columns[:, j : j + 1] - sums[j : j + 1], -jnp.inf)
            weights = (scores * jnp.exp(gap)).astype(BF16)
            inside[:, lanes] = jnp.dot(weights, v[:, lanes], preferred_element_type=F32)
            gated[:, lanes] = jax.nn.sigmoid(g[:, lanes].astype(F32)) * gains[j : j + 1]

    def many_inside(start, stop):
        def one(step, _):
            make_inside(step)
            return 0

        lax.fori_loop(start, stop, one, 0)

    def await_states(i):
        for d in range(1, ny):
            s_copy(i, d, lax.rem(y + ny - d, ny), lax.rem(y + d, ny)).wait_recv()

    def make_totals(i):
        for j in range(few):
            local = i * few + j
            total = s_in[0, local].astype(F32)
            for part in range(1, ny):
                total = total * step_decay[part, local : local + 1, :] + s_in[part, local].astype(F32)
            for n in range(pieces):
                b_out[i, j * pieces + n, :piece, :] = total[n * piece : (n + 1) * piece]
                b_out[i, j * pieces + n, piece:, :] = jnp.broadcast_to(
                    block_decay[local : local + 1, :], (PAD, DH)
                )
        for e in range(1, nzc):
            b_copy(i, e, zc, lax.rem(zc + e, nzc)).start()
        b_in[i, zc] = b_out[i, zc]

    def make_group_total(i):
        for e in range(1, nzc):
            b_copy(i, e, lax.rem(zc + nzc - e, nzc), lax.rem(zc + e, nzc)).wait_recv()
        total = b_in[i, 0, :piece, :]
        decay = b_in[i, 0, piece:, :]
        for block in range(1, nzc):
            step = b_in[i, block, piece:, :]
            total = total * step[:1] + b_in[i, block, :piece, :]
            decay = decay * step
        t_out[i, :piece, :] = total
        t_out[i, piece:, :] = decay
        for d in range(1, nx):

            @pl.when(x + d < nx)
            def _(d=d):
                t_copy(i, d).start()

    def make_carried(i):
        c_now[...] = jnp.zeros_like(c_now)
        for d in range(nx - 1, 0, -1):

            @pl.when(x >= d)
            def _(d=d):
                t_copy(i, d).wait_recv()
                c_now[...] = c_now[...] * t_in[i, d - 1, piece : piece + 1, :] + t_in[i, d - 1, :piece, :]

        state = c_now[...]
        for block in range(nzc):
            c_out[i, block] = state
            if block + 1 < nzc:
                state = state * b_in[i, block, piece : piece + 1, :] + b_in[i, block, :piece, :]
        for e in range(1, nzc):
            c_copy(i, e, zc, lax.rem(zc + e, nzc)).start()
        c_in[i, zc] = c_out[i, zc]

    def make_prefixes(i):
        for e in range(1, nzc):
            c_copy(i, e, lax.rem(zc + nzc - e, nzc), lax.rem(zc + e, nzc)).wait_recv()
        for j in range(few):
            local = i * few + j
            state = c_in[i, j * pieces : (j + 1) * pieces].reshape(DH, DH)
            for part in range(ny):
                p_out[part, local] = state.astype(BF16)
                if part + 1 < ny:
                    decay = step_decay[part, local : local + 1, :]
                    state = state * decay + s_in[part, local].astype(F32)
        for d in far_first:
            p_copy(i, d, y, lax.rem(y + d, ny)).start()
        there = pl.ds(i * few, few)
        p_in[y, there] = p_out[y, there]

    def make_outputs(i, d):
        group = lax.rem(y + ny - d, ny)
        if d:
            p_copy(i, d, group, lax.rem(y + d, ny)).wait_recv()
        begin = pl.multiple_of(group * per_owner, per_owner)
        first = begin + i * few
        columns = pltpu.roll(exp_col[...], lax.rem(DH - first, DH), axis=1)[:, :few]
        for j in range(few):
            lanes = lanes_of(first, j)
            from_state = jnp.dot(
                q[:, lanes], p_in[group, i * few + j], preferred_element_type=F32
            )
            mixed = inside[:, lanes] + columns[:, j : j + 1] * from_state
            scale = lax.rsqrt(jnp.mean(mixed * mixed, axis=1, keepdims=True) + 1e-6)
            o[:, lanes] = (mixed * scale * gated[:, lanes]).astype(BF16)
        store(i, d).start()

    def ready_rest():
        loads[4].wait()
        loads[5].wait()
        for d in range(1, ny):
            gain_copy(d, lax.rem(y + ny - d, ny)).wait_recv()
        for group in range(ny):
            gain[pl.ds(group * per_owner, per_owner), :] = gain_in[group].astype(F32)

    steps = heads // wide
    eighth = [steps * n // 8 for n in range(9)]

    def ins(n):
        many_inside(eighth[n], eighth[n + 1])

    loads[2].wait()
    loads[3].wait()
    make_states(0)
    send_states(0)
    make_states(1)
    ready_rest()
    ins(0)
    send_states(1)
    make_states(2)
    make_states(3)
    ins(1)
    await_states(0)
    send_states(2)
    make_totals(0)
    ins(2)
    await_states(1)
    send_states(3)
    make_totals(1)
    make_group_total(0)
    ins(3)
    make_carried(0)
    ins(4)
    make_group_total(1)
    make_prefixes(0)
    await_states(2)
    make_totals(2)
    make_carried(1)
    ins(5)
    make_group_total(2)
    make_prefixes(1)
    await_states(3)
    make_totals(3)
    make_carried(2)
    ins(6)
    make_group_total(3)
    make_prefixes(2)
    ins(7)
    make_carried(3)
    for d in [0] + far_first:
        make_outputs(0, d)
    make_prefixes(3)
    for i in range(1, chunks):
        for d in [0] + far_first:
            make_outputs(i, d)

    for d in range(1, ny):
        ld_copy(d, y).wait_send()
        gain_copy(d, y).wait_send()
    for i in range(chunks):
        for d in range(1, ny):
            s_copy(i, d, y, lax.rem(y + d, ny)).wait_send()
            p_copy(i, d, y, lax.rem(y + d, ny)).wait_send()
        for e in range(1, nzc):
            b_copy(i, e, zc, lax.rem(zc + e, nzc)).wait_send()
            c_copy(i, e, zc, lax.rem(zc + e, nzc)).wait_send()
        for d in range(1, nx):

            @pl.when(x + d < nx)
            def _(i=i, d=d):
                t_copy(i, d).wait_send()

        for d in range(ny):
            store(i, d).wait()


def on_device(dims, queries, keys, values, gate, log_decay, norm_gain):
    ny, nx, nzc, chunks, few = dims
    per_owner = chunks * few
    pieces = nzc // few
    piece = DH // pieces
    heads = ny * per_owner
    _, rows, width = queries.shape
    block = log_decay.shape[2]
    dma = pltpu.SemaphoreType.DMA
    vmem = pltpu.VMEM
    stream = [vmem((rows, width), BF16)] * 5
    out = pl.pallas_call(
        functools.partial(kernel, dims),
        out_shape=jax.ShapeDtypeStruct((rows, width), BF16),
        in_specs=[pl.BlockSpec(memory_space=pl.ANY)] * 6,
        out_specs=pl.BlockSpec(memory_space=pl.ANY),
        scratch_shapes=stream
        + [
            vmem((ny, per_owner, block), F32),
            vmem((ny, per_owner, DH), BF16),
            vmem((heads, DH), F32),
            vmem((heads, rows), F32),
            vmem((heads, rows), F32),
            vmem((rows, rows), F32),
            vmem((rows, rows), F32),
            vmem((ny, per_owner, DH), F32),
            vmem((per_owner, DH), F32),
            vmem((heads, DH, DH), BF16),
            vmem((ny, per_owner, DH, DH), BF16),
            vmem((chunks, nzc, piece + PAD, DH), F32),
            vmem((chunks, nzc, piece + PAD, DH), F32),
            vmem((chunks, piece + PAD, DH), F32),
            vmem((chunks, nx - 1, piece + PAD, DH), F32),
            vmem((piece, DH), F32),
            vmem((chunks, nzc, piece, DH), F32),
            vmem((chunks, nzc, piece, DH), F32),
            vmem((ny, per_owner, DH, DH), BF16),
            vmem((ny, per_owner, DH, DH), BF16),
            vmem((rows, width), F32),
            vmem((rows, width), F32),
            dma((6,)),
            dma((chunks, ny)),
            dma((ny - 1,)),
            dma((ny - 1,)),
            dma((ny - 1,)),
            dma((ny - 1,)),
            dma((chunks, ny - 1)),
            dma((chunks, ny - 1)),
            dma((chunks, nzc - 1)),
            dma((chunks, nzc - 1)),
            dma((chunks, nx - 1)),
            dma((chunks, nx - 1)),
            dma((chunks, nzc - 1)),
            dma((chunks, nzc - 1)),
            dma((chunks, ny - 1)),
            dma((chunks, ny - 1)),
        ],
        compiler_params=pltpu.CompilerParams(
            collective_id=0, has_side_effects=True, vmem_limit_bytes=52 * 2**20
        ),
        cost_estimate=pl.CostEstimate(
            flops=8 * rows * DH * width, bytes_accessed=10 * rows * width, transcendentals=0
        ),
    )(
        queries[0],
        keys[0],
        values[0],
        gate[0],
        log_decay[0],
        norm_gain.reshape(per_owner, DH),
    )
    return out[None]


def solution(mesh):
    ny = mesh.shape["head"]
    nctx = mesh.shape["ctx"]
    nx = 4 if nctx >= 16 else 2
    def whole(queries, keys, values, gate, log_decay, norm_gain):
        chunks = 4
        few = log_decay.shape[1] // (ny * chunks)
        dims = (ny, nx, nctx // nx, chunks, few)
        return jax.shard_map(
            functools.partial(on_device, dims),
            mesh=mesh,
            in_specs=(P("ctx", "head", None),) * 5 + (P("head"),),
            out_specs=P("ctx", "head", None),
            check_vma=False,
        )(queries, keys, values, gate, log_decay, norm_gain)

    return whole
```

```python
import functools

import jax
import jax.numpy as jnp
from jax import lax
from jax.experimental import pallas as pl
from jax.experimental.pallas import tpu as pltpu
from jax.sharding import PartitionSpec as P

MESH = pl.DeviceIdType.MESH
F32 = jnp.float32
BF16 = jnp.bfloat16
DH = 128
SCHEDULE = (
    "S0 s0 S1 r",
    "I s1 S2 S3",
    "I I I I",
    "W0 s2 T0 I",
    "I W1 s3 T1",
    "G0 I I K0",
    "I G1 I X0",
    "W2 T2 K1 I",
    "I G2 X1 I",
    "W3 T3 K2 I",
    "G3 X2 I K3",
    "O00 O02 O01 O03",
    "X3 O10 O12 O11",
    "O13 O20 O22 O21",
    "O23 O30 O32 O31",
    "O33",
)
PAD = 8
HIGHEST = lax.Precision.HIGHEST


def kernel(
    dims,
    q_hbm, k_hbm, v_hbm, g_hbm, ld_hbm, gain_hbm,
    o,
    q, k, v, g,
    ld, ld_mine, run_ld, gain_in, gain,
    cum_row, dec_row, cum_col, exp_col, run_decay, all_decay,
    s_out, s_in, b_out, b_in, t_out, t_in, c_now, c_out, c_in, p_out, p_in,
    inside, gated,
    load_sem,
    ld_send, ld_recv, other_send, other_recv, gain_send, gain_recv,
    s_send, s_recv, b_send, b_recv, t_send, t_recv, c_send, c_recv, p_send, p_recv,
):
    ny, nx, nz, chunks, few = dims
    rows = q.shape[0]
    per_owner = chunks * few
    heads = 2 * ny * per_owner
    pieces = nz // few
    runs = 2 * ny
    piece = DH // pieces
    y = lax.axis_index("head")
    ctx = lax.axis_index("ctx")
    x = ctx // (2 * nz)
    z = (ctx // 2) % nz
    core = ctx % 2

    def at(x, z, core):
        return {"ctx": (x * nz + z) * 2 + core}

    def load(n, src, dst):
        return pltpu.make_async_copy(src, dst, load_sem.at[n])

    loads = [
        load(0, ld_hbm, ld),
        load(1, gain_hbm, gain_in.at[y]),
        load(2, k_hbm, k),
        load(3, v_hbm, v),
        load(4, q_hbm, q),
        load(5, g_hbm, g),
    ]
    for one in loads:
        one.start()

    barrier = pltpu.get_barrier_semaphore()
    column = [(d, f) for d in (2, 1, 3, 0) for f in (0, 1) if d < ny and (d, f) != (0, 0)]

    def core_at(f):
        return 1 - core if f else core

    def column_peer(d, f):
        return {"head": lax.rem(y + d, ny), **at(x, z, core_at(f))}

    def nth(d, f):
        return 2 * d + f - 1

    peers = [column_peer(d, f) for d, f in column]
    peers += [at(x, lax.rem(z + e, nz), core) for e in range(1, nz)]
    peers += [at(lax.rem(x + d, nx), z, core) for d in range(1, nx)]
    for peer in peers:
        pl.semaphore_signal(barrier, inc=1, device_id=peer, device_id_type=MESH)
    pl.semaphore_wait(barrier, len(peers))

    def remote(src, dst, send, recv, peer):
        return pltpu.make_async_remote_copy(
            src_ref=src, dst_ref=dst, send_sem=send, recv_sem=recv,
            device_id=peer, device_id_type=MESH,
        )

    def ld_copy(d, source, reader):
        theirs = pl.ds(pl.multiple_of(reader * rows, rows), rows)
        return remote(
            ld.at[:, theirs], ld_mine.at[source], ld_send.at[d - 1], ld_recv.at[d - 1],
            {"head": lax.rem(y + d, ny)},
        )

    def gain_copy(d, source):
        peer = {"head": lax.rem(y + d, ny)}
        return remote(
            gain_in.at[source], gain_in.at[source], gain_send.at[d - 1], gain_recv.at[d - 1], peer
        )

    def other_copy(half, block):
        rows_of = pl.ds(pl.multiple_of(half * per_owner, per_owner), per_owner)
        return remote(
            ld.at[rows_of], run_ld.at[block], other_send.at[0], other_recv.at[0], column_peer(0, 1)
        )

    loads[0].wait()
    for d in range(1, ny):
        ld_copy(d, y, lax.rem(y + d, ny)).start()
    mine = pl.ds(pl.multiple_of(y * rows, rows), rows)
    other_copy(1 - core, core).start()
    loads[1].wait()
    for d in range(1, ny):
        gain_copy(d, y).start()
    ld_mine[y] = ld[:, mine]
    run_ld[core] = ld[pl.ds(pl.multiple_of(core * per_owner, per_owner), per_owner), :]
    for d in range(1, ny):
        ld_copy(d, lax.rem(y + ny - d, ny), y).wait_recv()

    upper = (
        lax.broadcasted_iota(jnp.int32, (rows, rows), 0)
        <= lax.broadcasted_iota(jnp.int32, (rows, rows), 1)
    ).astype(F32)
    cum_col[...] = jnp.zeros_like(cum_col)
    for group in range(ny):
        cumulative = jnp.dot(
            ld_mine[group], upper, precision=HIGHEST, preferred_element_type=F32
        )
        here = pl.ds(group * 2 * per_owner, 2 * per_owner)
        cum_row[here, :] = cumulative
        dec_row[here, :] = jnp.exp(cumulative[:, rows - 1 :] - cumulative)
        cum_col[here, :] = cumulative
    cum_col[...] = cum_col[...].T
    exp_col[...] = jnp.exp(cum_col[...])

    def make_decays():
        other_copy(core, 1 - core).wait_recv()
        whole = jnp.zeros((per_owner, 1), F32)
        for run in range(runs):
            part = run_ld[run // ny, :, run % ny * rows : (run % ny + 1) * rows]
            total = jnp.sum(part, axis=1, keepdims=True)
            run_decay[run] = jnp.broadcast_to(jnp.exp(total), (per_owner, DH))
            whole = whole + total
        all_decay[...] = jnp.broadcast_to(jnp.exp(whole), (per_owner, DH))

    def s_copy(i, d, f, source, group, half):
        first = (group * 2 + half) * per_owner + i * few
        there = pl.ds(i * few, few)
        return remote(
            s_out.at[pl.ds(first, few)], s_in.at[source, there],
            s_send.at[i, nth(d, f)], s_recv.at[i, nth(d, f)], column_peer(d, f),
        )

    def s_sent(i, d, f):
        return s_copy(i, d, f, core * ny + y, lax.rem(y + d, ny), core_at(f))

    def s_got(i, d, f):
        return s_copy(i, d, f, core_at(f) * ny + lax.rem(y + ny - d, ny), y, core)

    def b_copy(i, e, source, owner):
        return remote(
            b_out.at[i, owner], b_in.at[i, source], b_send.at[i, e - 1], b_recv.at[i, e - 1],
            at(x, owner, core),
        )

    def t_copy(i, d):
        return remote(
            t_out.at[i], t_in.at[i, d - 1], t_send.at[i, d - 1], t_recv.at[i, d - 1],
            at(lax.rem(x + d, nx), z, core),
        )

    def c_copy(i, e, source, chip):
        return remote(
            c_out.at[i, chip], c_in.at[i, source], c_send.at[i, e - 1], c_recv.at[i, e - 1],
            at(x, chip, core),
        )

    def p_copy(i, d, f, run, group, half):
        there = pl.ds(i * few, few)
        return remote(
            p_out.at[run, there], p_in.at[group * 2 + half, there],
            p_send.at[i, nth(d, f)], p_recv.at[i, nth(d, f)], column_peer(d, f),
        )

    def p_sent(i, d, f):
        return p_copy(i, d, f, core_at(f) * ny + lax.rem(y + d, ny), y, core)

    def p_got(i, d, f):
        return p_copy(i, d, f, core * ny + y, lax.rem(y + ny - d, ny), core_at(f))

    def lanes_of(first, j):
        return pl.ds(pl.multiple_of((first + j) * DH, DH), DH)

    z_order = [e for e in (2, 1, 3) if e < nz]

    def make_states(i):
        for d, f in column + [(0, 0)]:
            begin = pl.multiple_of(
                (lax.rem(y + d, ny) * 2 + core_at(f)) * per_owner, per_owner
            )
            decays = dec_row[pl.ds(begin, per_owner), :]
            for j in range(i * few, (i + 1) * few):
                lanes = lanes_of(begin, j)
                decayed = (k[:, lanes].T.astype(F32) * decays[j : j + 1]).astype(BF16)
                state = jnp.dot(decayed, v[:, lanes], preferred_element_type=F32).astype(BF16)
                if (d, f) == (0, 0):
                    s_in[core * ny + y, j] = state
                else:
                    s_out[begin + j] = state

    def send_states(i):
        for d, f in column:
            s_sent(i, d, f).start()

    causal = lax.broadcasted_iota(jnp.int32, (rows, rows), 0) >= lax.broadcasted_iota(
        jnp.int32, (rows, rows), 1
    )
    def make_inside(first, count):
        for head in range(first, first + count):
            lanes = slice(head * DH, (head + 1) * DH)
            scores = lax.dot_general(
                q[:, lanes], k[:, lanes], (((1,), (1,)), ((), ())), preferred_element_type=F32
            )
            gap = cum_col[:, head : head + 1] - cum_row[head : head + 1, :]
            weights = (scores * jnp.exp(jnp.where(causal, gap, -jnp.inf))).astype(BF16)
            inside[:, lanes] = jnp.dot(weights, v[:, lanes], preferred_element_type=F32)
            gated[:, lanes] = jax.nn.sigmoid(g[:, lanes].astype(F32)) * gain[head : head + 1, :]

    def await_states(i):
        for d, f in column:
            s_got(i, d, f).wait_recv()

    def make_totals(i):
        for j in range(few):
            local = i * few + j
            total = s_in[0, local].astype(F32)
            for run in range(1, runs):
                total = total * run_decay[run, local : local + 1, :] + s_in[run, local].astype(F32)
            for n in range(pieces):
                b_out[i, j * pieces + n, :piece, :] = total[n * piece : (n + 1) * piece]
                b_out[i, j * pieces + n, piece:, :] = jnp.broadcast_to(
                    all_decay[local : local + 1, :], (PAD, DH)
                )
        for e in z_order:
            b_copy(i, e, z, lax.rem(z + e, nz)).start()
        b_in[i, z] = b_out[i, z]

    def make_group_total(i):
        for e in range(1, nz):
            b_copy(i, e, lax.rem(z + nz - e, nz), lax.rem(z + e, nz)).wait_recv()
        total = b_in[i, 0, :piece, :]
        decay = b_in[i, 0, piece:, :]
        for chip in range(1, nz):
            step = b_in[i, chip, piece:, :]
            total = total * step[:1] + b_in[i, chip, :piece, :]
            decay = decay * step
        t_out[i, :piece, :] = total
        t_out[i, piece:, :] = decay
        for d in range(1, nx):

            @pl.when(x + d < nx)
            def _(d=d):
                t_copy(i, d).start()

    def make_carried(i):
        c_now[...] = jnp.zeros_like(c_now)
        for d in range(nx - 1, 0, -1):

            @pl.when(x >= d)
            def _(d=d):
                t_copy(i, d).wait_recv()
                c_now[...] = c_now[...] * t_in[i, d - 1, piece : piece + 1, :] + t_in[i, d - 1, :piece, :]

        state = c_now[...]
        for chip in range(nz):
            c_out[i, chip] = state
            if chip + 1 < nz:
                state = state * b_in[i, chip, piece : piece + 1, :] + b_in[i, chip, :piece, :]
        for e in z_order:
            c_copy(i, e, z, lax.rem(z + e, nz)).start()
        c_in[i, z] = c_out[i, z]

    def make_prefixes(i):
        for e in range(1, nz):
            c_copy(i, e, lax.rem(z + nz - e, nz), lax.rem(z + e, nz)).wait_recv()
        for j in range(few):
            local = i * few + j
            state = c_in[i, j * pieces : (j + 1) * pieces].reshape(DH, DH)
            for run in range(runs):
                p_out[run, local] = state.astype(BF16)
                if run + 1 < runs:
                    decay = run_decay[run, local : local + 1, :]
                    state = state * decay + s_in[run, local].astype(F32)
        for d, f in column:
            p_sent(i, d, f).start()
        there = pl.ds(i * few, few)
        p_in[y * 2 + core, there] = p_out[core * ny + y, there]

    def make_outputs(i, d):
        group = lax.rem(y + ny - d, ny)
        for f in (0, 1):
            if (d, f) in column:
                p_got(i, d, f).wait_recv()
        for half in (0, 1):
            first = (group * 2 + half) * per_owner + i * few
            columns = pltpu.roll(exp_col[...], lax.rem(DH - first, DH), axis=1)[:, :few]
            for j in range(few):
                lanes = lanes_of(first, j)
                from_state = jnp.dot(
                    q[:, lanes], p_in[group * 2 + half, i * few + j], preferred_element_type=F32
                )
                mixed = inside[:, lanes] + columns[:, j : j + 1] * from_state
                scale = lax.rsqrt(jnp.mean(mixed * mixed, axis=1, keepdims=True) + 1e-6)
                o[:, lanes] = (mixed * scale * gated[:, lanes]).astype(BF16)

    def ready_rest():
        loads[4].wait()
        loads[5].wait()
        for d in range(1, ny):
            gain_copy(d, lax.rem(y + ny - d, ny)).wait_recv()
        for group in range(ny):
            gain[pl.ds(group * 2 * per_owner, 2 * per_owner), :] = gain_in[group].astype(F32)
        make_decays()

    sixteenth = heads // 16
    loads[2].wait()
    loads[3].wait()
    plan = " ".join(SCHEDULE).split()
    inner = iter(range(16))
    calls = dict(
        S=make_states, s=send_states, W=await_states, T=make_totals,
        G=make_group_total, K=make_carried, X=make_prefixes,
    )
    for word in plan:
        if word == "r":
            ready_rest()
        elif word == "I":
            make_inside(next(inner) * sixteenth, sixteenth)
        elif word[0] == "O":
            make_outputs(int(word[1]), int(word[2]))
        else:
            calls[word[0]](int(word[1]))

    for d in range(1, ny):
        ld_copy(d, y, lax.rem(y + d, ny)).wait_send()
        gain_copy(d, y).wait_send()
    other_copy(1 - core, core).wait_send()
    for i in range(chunks):
        for d, f in column:
            s_sent(i, d, f).wait_send()
            p_sent(i, d, f).wait_send()
        for e in range(1, nz):
            b_copy(i, e, z, lax.rem(z + e, nz)).wait_send()
            c_copy(i, e, z, lax.rem(z + e, nz)).wait_send()
        for d in range(1, nx):

            @pl.when(x + d < nx)
            def _(i=i, d=d):
                t_copy(i, d).wait_send()


def on_device(dims, queries, keys, values, gate, log_decay, norm_gain):
    ny, nx, nz, chunks, few = dims
    per_owner = chunks * few
    piece = DH * few // nz
    runs = 2 * ny
    heads = runs * per_owner
    _, rows, width = queries.shape
    block = log_decay.shape[2]
    dma = pltpu.SemaphoreType.DMA
    vmem = pltpu.VMEM
    stream = [vmem((rows, width), BF16)] * 4
    out = pl.pallas_call(
        functools.partial(kernel, dims),
        out_shape=pltpu.VMEM((rows, width), BF16),
        in_specs=[pl.BlockSpec(memory_space=pltpu.HBM)] * 6,
        out_specs=pl.BlockSpec(memory_space=pltpu.VMEM),
        scratch_shapes=stream
        + [
            vmem((2 * per_owner, block), F32),
            vmem((ny, 2 * per_owner, rows), F32),
            vmem((2, per_owner, block), F32),
            vmem((ny, 2 * per_owner, DH), BF16),
            vmem((heads, DH), F32),
            vmem((heads, rows), F32),
            vmem((heads, rows), F32),
            vmem((rows, rows), F32),
            vmem((rows, rows), F32),
            vmem((runs, per_owner, DH), F32),
            vmem((per_owner, DH), F32),
            vmem((heads, DH, DH), BF16),
            vmem((runs, per_owner, DH, DH), BF16),
            vmem((chunks, nz, piece + PAD, DH), F32),
            vmem((chunks, nz, piece + PAD, DH), F32),
            vmem((chunks, piece + PAD, DH), F32),
            vmem((chunks, nx - 1, piece + PAD, DH), F32),
            vmem((piece, DH), F32),
            vmem((chunks, nz, piece, DH), F32),
            vmem((chunks, nz, piece, DH), F32),
            vmem((runs, per_owner, DH, DH), BF16),
            vmem((runs, per_owner, DH, DH), BF16),
            vmem((rows, width), F32),
            vmem((rows, width), F32),
            dma((6,)),
            dma((ny - 1,)),
            dma((ny - 1,)),
            dma((1,)),
            dma((1,)),
            dma((ny - 1,)),
            dma((ny - 1,)),
            dma((chunks, runs - 1)),
            dma((chunks, runs - 1)),
            dma((chunks, nz - 1)),
            dma((chunks, nz - 1)),
            dma((chunks, nx - 1)),
            dma((chunks, nx - 1)),
            dma((chunks, nz - 1)),
            dma((chunks, nz - 1)),
            dma((chunks, runs - 1)),
            dma((chunks, runs - 1)),
        ],
        compiler_params=pltpu.CompilerParams(
            collective_id=0, has_side_effects=True, vmem_limit_bytes=52 * 2**20
        ),
        cost_estimate=pl.CostEstimate(
            flops=8 * rows * DH * width, bytes_accessed=10 * rows * width, transcendentals=0
        ),
    )(
        queries[0],
        keys[0],
        values[0],
        gate[0],
        log_decay[0],
        norm_gain.reshape(2 * per_owner, DH),
    )
    return out[None]


def solution(mesh):
    ny = mesh.shape["head"]
    nctx = mesh.shape["ctx"]
    nx = 4 if nctx >= 16 else 2
    def whole(queries, keys, values, gate, log_decay, norm_gain):
        chunks = 4
        few = log_decay.shape[1] // (2 * ny * chunks)
        dims = (ny, nx, nctx // (2 * nx), chunks, few)
        return jax.shard_map(
            functools.partial(on_device, dims),
            mesh=mesh,
            in_specs=(P("ctx", "head", None),) * 5 + (P("head"),),
            out_specs=P("ctx", "head", None),
            check_vma=False,
        )(queries, keys, values, gate, log_decay, norm_gain)

    return whole
```

```python
import functools

import jax
import jax.numpy as jnp
from jax import lax
from jax.experimental import pallas as pl
from jax.experimental.pallas import tpu as pltpu
from jax.sharding import PartitionSpec as P

MESH = pl.DeviceIdType.MESH
F32 = jnp.float32
BF16 = jnp.bfloat16
DH = 128
CHUNKS = 4
SCHEDULE = (
    "F0 S1 r I",
    "s1 S2 S3 I",
    "I I I A0",
    "W0 s2 T0 I",
    "I W1 s3 T1",
    "G0 I I K0",
    "I G1 I X0",
    "W2 T2 K1 I",
    "I G2 X1 I",
    "W3 T3 K2 I",
    "G3 X2 I K3",
    "U0 U1 O00 O02",
    "O01 O03 X3 U2",
    "M0 M1 O10 O12",
    "O11 O13 P0 U3",
    "M2 M3 O20 O22",
    "O21 O23 P1 P2",
    "O30 O32 O31 O33",
    "P3",
)
PAD = 8
HIGHEST = lax.Precision.HIGHEST


def kernel(
    dims,
    q_hbm, k_hbm, v_hbm, g_hbm, ld_hbm, gain_hbm,
    o,
    q, k, v, g,
    ld, ld_mine, run_ld, gain_in, gain,
    cum_row, dec_row, cum_col, exp_col, run_decay, all_decay,
    s_out, s_in, b_out, b_in, t_out, t_in, c_now, c_out, c_in, p_out, p_in,
    inside, gated,
    load_sem,
    ld_send, ld_recv, other_send, other_recv, gain_send, gain_recv,
    s_send, s_recv, b_send, b_recv, t_send, t_recv, c_send, c_recv, p_send, p_recv,
):
    ny, nx, nz, chunks, few = dims
    rows = q.shape[0]
    per_owner = chunks * few
    heads = 2 * ny * per_owner
    pieces = nz // few
    runs = 2 * ny
    piece = DH // pieces
    y = lax.axis_index("head")
    ctx = lax.axis_index("ctx")
    x = ctx // (2 * nz)
    z = (ctx // 2) % nz
    core = ctx % 2

    def at(x, z, core):
        return {"ctx": (x * nz + z) * 2 + core}

    def load(n, src, dst):
        return pltpu.make_async_copy(src, dst, load_sem.at[n])

    loads = [
        load(0, ld_hbm, ld),
        load(1, gain_hbm, gain_in.at[y]),
        load(2, k_hbm, k),
        load(3, v_hbm, v),
        load(4, q_hbm, q),
        load(5, g_hbm, g),
    ]
    for one in loads:
        one.start()

    barrier = pltpu.get_barrier_semaphore()
    column = [(d, f) for d in (2, 1, 3, 0) for f in (0, 1) if d < ny and (d, f) != (0, 0)]

    def core_at(f):
        return 1 - core if f else core

    def column_peer(d, f):
        return {"head": lax.rem(y + d, ny), **at(x, z, core_at(f))}

    def nth(d, f):
        return 2 * d + f - 1

    peers = [column_peer(d, f) for d, f in column]
    peers += [at(x, lax.rem(z + e, nz), core) for e in range(1, nz)]
    peers += [at(lax.rem(x + d, nx), z, core) for d in range(1, nx)]
    for peer in peers:
        pl.semaphore_signal(barrier, inc=1, device_id=peer, device_id_type=MESH)
    pl.semaphore_wait(barrier, len(peers))

    def remote(src, dst, send, recv, peer):
        return pltpu.make_async_remote_copy(
            src_ref=src, dst_ref=dst, send_sem=send, recv_sem=recv,
            device_id=peer, device_id_type=MESH,
        )

    def ld_copy(d, source, reader):
        theirs = pl.ds(pl.multiple_of(reader * rows, rows), rows)
        return remote(
            ld.at[:, theirs], ld_mine.at[source], ld_send.at[d - 1], ld_recv.at[d - 1],
            {"head": lax.rem(y + d, ny)},
        )

    def gain_copy(d, source):
        peer = {"head": lax.rem(y + d, ny)}
        return remote(
            gain_in.at[source], gain_in.at[source], gain_send.at[d - 1], gain_recv.at[d - 1], peer
        )

    def other_copy(half, block):
        rows_of = pl.ds(pl.multiple_of(half * per_owner, per_owner), per_owner)
        return remote(
            ld.at[rows_of], run_ld.at[block], other_send.at[0], other_recv.at[0], column_peer(0, 1)
        )

    loads[0].wait()
    for d in range(1, ny):
        ld_copy(d, y, lax.rem(y + d, ny)).start()
    mine = pl.ds(pl.multiple_of(y * rows, rows), rows)
    other_copy(1 - core, core).start()
    loads[1].wait()
    for d in range(1, ny):
        gain_copy(d, y).start()
    ld_mine[y] = ld[:, mine]
    run_ld[core] = ld[pl.ds(pl.multiple_of(core * per_owner, per_owner), per_owner), :]
    for d in range(1, ny):
        ld_copy(d, lax.rem(y + ny - d, ny), y).wait_recv()

    upper = (
        lax.broadcasted_iota(jnp.int32, (rows, rows), 0)
        <= lax.broadcasted_iota(jnp.int32, (rows, rows), 1)
    ).astype(F32)
    for group in range(ny):
        cumulative = jnp.dot(
            ld_mine[group], upper, precision=HIGHEST, preferred_element_type=F32
        )
        here = pl.ds(group * 2 * per_owner, 2 * per_owner)
        cum_row[here, :] = cumulative
        dec_row[here, :] = jnp.exp(cumulative[:, rows - 1 :] - cumulative)

    def make_columns():
        cum_col[:heads, :] = cum_row[...]
        if heads < rows:
            cum_col[heads:, :] = jnp.zeros((rows - heads, rows), F32)
        cum_col[...] = cum_col[...].T
        exp_col[...] = jnp.exp(cum_col[...])

    def make_decays():
        other_copy(core, 1 - core).wait_recv()
        whole = jnp.zeros((per_owner, 1), F32)
        for run in range(runs):
            part = run_ld[run // ny, :, run % ny * rows : (run % ny + 1) * rows]
            total = jnp.sum(part, axis=1, keepdims=True)
            run_decay[run] = jnp.broadcast_to(jnp.exp(total), (per_owner, DH))
            whole = whole + total
        all_decay[...] = jnp.broadcast_to(jnp.exp(whole), (per_owner, DH))

    def s_copy(i, d, f, source, group, half):
        first = (group * 2 + half) * per_owner + i * few
        there = pl.ds(i * few, few)
        return remote(
            s_out.at[pl.ds(first, few)], s_in.at[source, there],
            s_send.at[i, nth(d, f)], s_recv.at[i, nth(d, f)], column_peer(d, f),
        )

    def s_sent(i, d, f):
        return s_copy(i, d, f, core * ny + y, lax.rem(y + d, ny), core_at(f))

    def s_got(i, d, f):
        return s_copy(i, d, f, core_at(f) * ny + lax.rem(y + ny - d, ny), y, core)

    def b_copy(i, e, source, owner):
        return remote(
            b_out.at[i, owner], b_in.at[i, source], b_send.at[i, e - 1], b_recv.at[i, e - 1],
            at(x, owner, core),
        )

    def t_copy(i, d):
        return remote(
            t_out.at[i], t_in.at[i, d - 1], t_send.at[i, d - 1], t_recv.at[i, d - 1],
            at(lax.rem(x + d, nx), z, core),
        )

    def c_copy(i, e, source, chip):
        return remote(
            c_out.at[i, chip], c_in.at[i, source], c_send.at[i, e - 1], c_recv.at[i, e - 1],
            at(x, chip, core),
        )

    def p_copy(i, d, f, run, group, half):
        there = pl.ds(i * few, few)
        return remote(
            p_out.at[run, there], p_in.at[group * 2 + half, there],
            p_send.at[i, nth(d, f)], p_recv.at[i, nth(d, f)], column_peer(d, f),
        )

    def p_sent(i, d, f):
        return p_copy(i, d, f, core_at(f) * ny + lax.rem(y + d, ny), y, core)

    def p_got(i, d, f):
        return p_copy(i, d, f, core * ny + y, lax.rem(y + ny - d, ny), core_at(f))

    def lanes_of(first, j):
        return pl.ds(pl.multiple_of((first + j) * DH, DH), DH)

    z_order = [e for e in (2, 1, 3) if e < nz]

    def make_states(i, send=False):
        for d, f in column + [(0, 0)]:
            begin = pl.multiple_of(
                (lax.rem(y + d, ny) * 2 + core_at(f)) * per_owner, per_owner
            )
            decays = dec_row[pl.ds(begin, per_owner), :]
            for j in range(i * few, (i + 1) * few):
                lanes = lanes_of(begin, j)
                decayed = (k[:, lanes].T.astype(F32) * decays[j : j + 1]).astype(BF16)
                state = jnp.dot(decayed, v[:, lanes], preferred_element_type=F32).astype(BF16)
                if (d, f) == (0, 0):
                    s_in[core * ny + y, j] = state
                else:
                    s_out[begin + j] = state
            if send and (d, f) != (0, 0):
                s_sent(i, d, f).start()

    def send_states(i):
        for d, f in column:
            s_sent(i, d, f).start()

    causal = lax.broadcasted_iota(jnp.int32, (rows, rows), 0) >= lax.broadcasted_iota(
        jnp.int32, (rows, rows), 1
    )
    def make_inside(first, count):
        for head in range(first, first + count):
            lanes = slice(head * DH, (head + 1) * DH)
            scores = lax.dot_general(
                q[:, lanes], k[:, lanes], (((1,), (1,)), ((), ())), preferred_element_type=F32
            )
            gap = cum_col[:, head : head + 1] - cum_row[head : head + 1, :]
            weights = (scores * jnp.exp(jnp.where(causal, gap, -jnp.inf))).astype(BF16)
            inside[:, lanes] = jnp.dot(weights, v[:, lanes], preferred_element_type=F32)
            gated[:, lanes] = jax.nn.sigmoid(g[:, lanes].astype(F32)) * gain[head : head + 1, :]

    def await_states(i):
        for d, f in column:
            s_got(i, d, f).wait_recv()

    def make_totals(i):
        for j in range(few):
            local = i * few + j
            total = s_in[0, local].astype(F32)
            for run in range(1, runs):
                total = total * run_decay[run, local : local + 1, :] + s_in[run, local].astype(F32)
            for n in range(pieces):
                b_out[i, j * pieces + n, :piece, :] = total[n * piece : (n + 1) * piece]
                b_out[i, j * pieces + n, piece:, :] = jnp.broadcast_to(
                    all_decay[local : local + 1, :], (PAD, DH)
                )
        for e in z_order:
            b_copy(i, e, z, lax.rem(z + e, nz)).start()
        b_in[i, z] = b_out[i, z]

    def make_group_total(i):
        for e in range(1, nz):
            b_copy(i, e, lax.rem(z + nz - e, nz), lax.rem(z + e, nz)).wait_recv()
        total = b_in[i, 0, :piece, :]
        decay = b_in[i, 0, piece:, :]
        for chip in range(1, nz):
            step = b_in[i, chip, piece:, :]
            total = total * step[:1] + b_in[i, chip, :piece, :]
            decay = decay * step
        t_out[i, :piece, :] = total
        t_out[i, piece:, :] = decay
        for d in range(1, nx):

            @pl.when(x + d < nx)
            def _(d=d):
                t_copy(i, d).start()

    def make_carried(i):
        c_now[...] = jnp.zeros_like(c_now)
        for d in range(nx - 1, 0, -1):

            @pl.when(x >= d)
            def _(d=d):
                t_copy(i, d).wait_recv()
                c_now[...] = c_now[...] * t_in[i, d - 1, piece : piece + 1, :] + t_in[i, d - 1, :piece, :]

        state = c_now[...]
        for chip in range(nz):
            c_out[i, chip] = state
            if chip + 1 < nz:
                state = state * b_in[i, chip, piece : piece + 1, :] + b_in[i, chip, :piece, :]
        for e in z_order:
            c_copy(i, e, z, lax.rem(z + e, nz)).start()
        c_in[i, z] = c_out[i, z]

    def make_prefixes(i):
        for e in range(1, nz):
            c_copy(i, e, lax.rem(z + nz - e, nz), lax.rem(z + e, nz)).wait_recv()
        for j in range(few):
            local = i * few + j
            state = c_in[i, j * pieces : (j + 1) * pieces].reshape(DH, DH)
            for run in range(runs):
                p_out[run, local] = state.astype(BF16)
                if run + 1 < runs:
                    decay = run_decay[run, local : local + 1, :]
                    state = state * decay + s_in[run, local].astype(F32)
        for d, f in column:
            p_sent(i, d, f).start()
        there = pl.ds(i * few, few)
        p_in[y * 2 + core, there] = p_out[core * ny + y, there]

    def make_outputs(i, d):
        group = lax.rem(y + ny - d, ny)
        for f in (0, 1):
            if (d, f) in column:
                p_got(i, d, f).wait_recv()
        for half in (0, 1):
            first = (group * 2 + half) * per_owner + i * few
            columns = pltpu.roll(exp_col[...], lax.rem(DH - first, DH), axis=1)[:, :few]
            for j in range(few):
                lanes = lanes_of(first, j)
                from_state = jnp.dot(
                    q[:, lanes], p_in[group * 2 + half, i * few + j], preferred_element_type=F32
                )
                mixed = inside[:, lanes] + columns[:, j : j + 1] * from_state
                scale = lax.rsqrt(jnp.mean(mixed * mixed, axis=1, keepdims=True) + 1e-6)
                o[:, lanes] = (mixed * scale * gated[:, lanes]).astype(BF16)

    def ready_rest():
        loads[4].wait()
        loads[5].wait()
        for d in range(1, ny):
            gain_copy(d, lax.rem(y + ny - d, ny)).wait_recv()
        for group in range(ny):
            gain[pl.ds(group * 2 * per_owner, 2 * per_owner), :] = gain_in[group].astype(F32)
        make_columns()
        make_decays()

    def drain_first(_):
        for d in range(1, ny):
            ld_copy(d, y, lax.rem(y + d, ny)).wait_send()
            gain_copy(d, y).wait_send()
        other_copy(1 - core, core).wait_send()

    def drain_up(i):
        for d, f in column:
            s_sent(i, d, f).wait_send()
        for e in range(1, nz):
            b_copy(i, e, z, lax.rem(z + e, nz)).wait_send()

    def drain_middle(i):
        for e in range(1, nz):
            c_copy(i, e, z, lax.rem(z + e, nz)).wait_send()
        for d in range(1, nx):

            @pl.when(x + d < nx)
            def _(d=d):
                t_copy(i, d).wait_send()

    def drain_down(i):
        for d, f in column:
            p_sent(i, d, f).wait_send()

    sixteenth = heads // 16
    loads[2].wait()
    loads[3].wait()
    plan = " ".join(SCHEDULE).split()
    inner = iter(range(16))
    calls = dict(
        S=make_states, s=send_states, F=functools.partial(make_states, send=True), W=await_states, T=make_totals,
        G=make_group_total, K=make_carried, X=make_prefixes,
        A=drain_first, U=drain_up, M=drain_middle, P=drain_down,
    )
    for word in plan:
        if word == "r":
            ready_rest()
        elif word == "I":
            make_inside(next(inner) * sixteenth, sixteenth)
        elif word[0] == "O":
            make_outputs(int(word[1]), int(word[2]))
        else:
            calls[word[0]](int(word[1]))


def on_device(dims, queries, keys, values, gate, log_decay, norm_gain):
    ny, nx, nz, chunks, few = dims
    per_owner = chunks * few
    piece = DH * few // nz
    runs = 2 * ny
    heads = runs * per_owner
    _, rows, width = queries.shape
    block = log_decay.shape[2]
    dma = pltpu.SemaphoreType.DMA
    vmem = pltpu.VMEM
    stream = [vmem((rows, width), BF16)] * 4
    out = pl.pallas_call(
        functools.partial(kernel, dims),
        out_shape=pltpu.VMEM((rows, width), BF16),
        in_specs=[pl.BlockSpec(memory_space=pltpu.HBM)] * 6,
        out_specs=pl.BlockSpec(memory_space=pltpu.VMEM),
        scratch_shapes=stream
        + [
            vmem((2 * per_owner, block), F32),
            vmem((ny, 2 * per_owner, rows), F32),
            vmem((2, per_owner, block), F32),
            vmem((ny, 2 * per_owner, DH), BF16),
            vmem((heads, DH), F32),
            vmem((heads, rows), F32),
            vmem((heads, rows), F32),
            vmem((rows, rows), F32),
            vmem((rows, rows), F32),
            vmem((runs, per_owner, DH), F32),
            vmem((per_owner, DH), F32),
            vmem((heads, DH, DH), BF16),
            vmem((runs, per_owner, DH, DH), BF16),
            vmem((chunks, nz, piece + PAD, DH), F32),
            vmem((chunks, nz, piece + PAD, DH), F32),
            vmem((chunks, piece + PAD, DH), F32),
            vmem((chunks, nx - 1, piece + PAD, DH), F32),
            vmem((piece, DH), F32),
            vmem((chunks, nz, piece, DH), F32),
            vmem((chunks, nz, piece, DH), F32),
            vmem((runs, per_owner, DH, DH), BF16),
            vmem((runs, per_owner, DH, DH), BF16),
            vmem((rows, width), F32),
            vmem((rows, width), F32),
            dma((6,)),
            dma((ny - 1,)),
            dma((ny - 1,)),
            dma((1,)),
            dma((1,)),
            dma((ny - 1,)),
            dma((ny - 1,)),
            dma((chunks, runs - 1)),
            dma((chunks, runs - 1)),
            dma((chunks, nz - 1)),
            dma((chunks, nz - 1)),
            dma((chunks, nx - 1)),
            dma((chunks, nx - 1)),
            dma((chunks, nz - 1)),
            dma((chunks, nz - 1)),
            dma((chunks, runs - 1)),
            dma((chunks, runs - 1)),
        ],
        compiler_params=pltpu.CompilerParams(
            collective_id=0, has_side_effects=True, vmem_limit_bytes=52 * 2**20
        ),
        cost_estimate=pl.CostEstimate(
            flops=8 * rows * DH * width, bytes_accessed=10 * rows * width, transcendentals=0
        ),
    )(
        queries[0],
        keys[0],
        values[0],
        gate[0],
        log_decay[0],
        norm_gain.reshape(2 * per_owner, DH),
    )
    return out[None]


def solution(mesh):
    ny = mesh.shape["head"]
    nctx = mesh.shape["ctx"]
    nx = 4 if nctx >= 16 else 2
    def whole(queries, keys, values, gate, log_decay, norm_gain):
        chunks = CHUNKS
        few = log_decay.shape[1] // (2 * ny * chunks)
        dims = (ny, nx, nctx // (2 * nx), chunks, few)
        return jax.shard_map(
            functools.partial(on_device, dims),
            mesh=mesh,
            in_specs=(P("ctx", "head", None),) * 5 + (P("head"),),
            out_specs=P("ctx", "head", None),
            check_vma=False,
        )(queries, keys, values, gate, log_decay, norm_gain)

    return whole
```

```python
import functools

import jax
import jax.numpy as jnp
from jax import lax
from jax.experimental import pallas as pl
from jax.experimental.pallas import tpu as pltpu
from jax.sharding import PartitionSpec as P

MESH = pl.DeviceIdType.MESH
F32 = jnp.float32
BF16 = jnp.bfloat16
DH = 128
CHUNKS = 4
SCHEDULE = (
    "F0 S1 r I",
    "s1 S2 S3 I",
    "I I I A0",
    "W0 s2 T0 I",
    "I W1 s3 T1",
    "G0 I I K0",
    "I G1 I X0",
    "W2 T2 K1 I",
    "I G2 X1 I",
    "W3 T3 K2 I",
    "G3 X2 I K3",
    "U0 U1 O00 O02",
    "O01 O03 X3 U2",
    "M0 M1 O10 O12",
    "O11 O13 P0 U3",
    "M2 M3 O20 O22",
    "O21 O23 P1 P2",
    "O30 O32 O31 O33",
    "P3",
)
PAD = 8
HIGHEST = lax.Precision.HIGHEST


def kernel(
    dims,
    q_hbm, k_hbm, v_hbm, g_hbm, ld_hbm, gain_hbm,
    o,
    q, k, v, g,
    ld, ld_mine, run_ld, gain_in, gain,
    cum_row, dec_row, cum_col, exp_col, run_decay, all_decay,
    s_out, s_in, b_out, b_in, t_out, t_in, c_now, c_out, c_in, p_out, p_in,
    inside, gated,
    load_sem,
    ld_send, ld_recv, other_send, other_recv, gain_send, gain_recv,
    s_send, s_recv, b_send, b_recv, t_send, t_recv, c_send, c_recv, p_send, p_recv,
):
    ny, nx, nz, chunks, few = dims
    rows = q.shape[0]
    per_owner = chunks * few
    heads = 2 * ny * per_owner
    pieces = nz // few
    runs = 2 * ny
    piece = DH // pieces
    y = lax.axis_index("head")
    ctx = lax.axis_index("ctx")
    x = ctx // (2 * nz)
    z = (ctx // 2) % nz
    core = ctx % 2

    def at(x, z, core):
        return {"ctx": (x * nz + z) * 2 + core}

    def load(n, src, dst):
        return pltpu.make_async_copy(src, dst, load_sem.at[n])

    loads = [
        load(0, ld_hbm, ld),
        load(1, gain_hbm, gain_in.at[y]),
        load(2, k_hbm, k),
        load(3, v_hbm, v),
        load(4, q_hbm, q),
        load(5, g_hbm, g),
    ]
    for one in loads:
        one.start()

    barrier = pltpu.get_barrier_semaphore()
    column = [(d, f) for d in (2, 1, 3, 0) for f in (0, 1) if d < ny and (d, f) != (0, 0)]

    def core_at(f):
        return 1 - core if f else core

    def column_peer(d, f):
        return {"head": lax.rem(y + d, ny), **at(x, z, core_at(f))}

    def nth(d, f):
        return 2 * d + f - 1

    peers = [column_peer(d, f) for d, f in column]
    peers += [at(x, lax.rem(z + e, nz), core) for e in range(1, nz)]
    peers += [at(lax.rem(x + d, nx), z, core) for d in range(1, nx)]
    for peer in peers:
        pl.semaphore_signal(barrier, inc=1, device_id=peer, device_id_type=MESH)
    pl.semaphore_wait(barrier, len(peers))

    def remote(src, dst, send, recv, peer):
        return pltpu.make_async_remote_copy(
            src_ref=src, dst_ref=dst, send_sem=send, recv_sem=recv,
            device_id=peer, device_id_type=MESH,
        )

    def ld_copy(d, source, reader):
        theirs = pl.ds(pl.multiple_of(reader * rows, rows), rows)
        return remote(
            ld.at[:, theirs], ld_mine.at[source], ld_send.at[d - 1], ld_recv.at[d - 1],
            {"head": lax.rem(y + d, ny)},
        )

    def gain_copy(d, source):
        peer = {"head": lax.rem(y + d, ny)}
        return remote(
            gain_in.at[source], gain_in.at[source], gain_send.at[d - 1], gain_recv.at[d - 1], peer
        )

    def other_copy(half, block):
        rows_of = pl.ds(pl.multiple_of(half * per_owner, per_owner), per_owner)
        return remote(
            ld.at[rows_of], run_ld.at[block], other_send.at[0], other_recv.at[0], column_peer(0, 1)
        )

    loads[0].wait()
    for d in [d for d in (2, 1, 3) if d < ny]:
        ld_copy(d, y, lax.rem(y + d, ny)).start()
    mine = pl.ds(pl.multiple_of(y * rows, rows), rows)
    other_copy(1 - core, core).start()
    loads[1].wait()
    for d in range(1, ny):
        gain_copy(d, y).start()
    ld_mine[y] = ld[:, mine]
    run_ld[core] = ld[pl.ds(pl.multiple_of(core * per_owner, per_owner), per_owner), :]
    upper = (
        lax.broadcasted_iota(jnp.int32, (rows, rows), 0)
        <= lax.broadcasted_iota(jnp.int32, (rows, rows), 1)
    ).astype(F32)
    loads[2].wait()
    loads[3].wait()
    for d in range(1, ny):
        ld_copy(d, lax.rem(y + ny - d, ny), y).wait_recv()

    cumulative = jnp.dot(
        ld_mine[...].reshape(heads, rows), upper, precision=HIGHEST, preferred_element_type=F32
    )
    dec_row[...] = jnp.exp(cumulative[:, rows - 1 :] - cumulative)
    cum_row[...] = cumulative

    def make_columns():
        cum_col[:heads, :] = cum_row[...]
        if heads < rows:
            cum_col[heads:, :] = jnp.zeros((rows - heads, rows), F32)
        cum_col[...] = cum_col[...].T
        exp_col[...] = jnp.exp(cum_col[...])

    def make_decays():
        other_copy(core, 1 - core).wait_recv()
        whole = jnp.zeros((per_owner, 1), F32)
        for run in range(runs):
            part = run_ld[run // ny, :, run % ny * rows : (run % ny + 1) * rows]
            total = jnp.sum(part, axis=1, keepdims=True)
            run_decay[run] = jnp.broadcast_to(jnp.exp(total), (per_owner, DH))
            whole = whole + total
        all_decay[...] = jnp.broadcast_to(jnp.exp(whole), (per_owner, DH))

    def s_copy(i, d, f, source, group, half):
        first = (group * 2 + half) * per_owner + i * few
        there = pl.ds(i * few, few)
        return remote(
            s_out.at[pl.ds(first, few)], s_in.at[source, there],
            s_send.at[i, nth(d, f)], s_recv.at[i, nth(d, f)], column_peer(d, f),
        )

    def s_sent(i, d, f):
        return s_copy(i, d, f, core * ny + y, lax.rem(y + d, ny), core_at(f))

    def s_got(i, d, f):
        return s_copy(i, d, f, core_at(f) * ny + lax.rem(y + ny - d, ny), y, core)

    def b_copy(i, e, source, owner):
        return remote(
            b_out.at[i, owner], b_in.at[i, source], b_send.at[i, e - 1], b_recv.at[i, e - 1],
            at(x, owner, core),
        )

    def t_copy(i, d):
        return remote(
            t_out.at[i], t_in.at[i, d - 1], t_send.at[i, d - 1], t_recv.at[i, d - 1],
            at(lax.rem(x + d, nx), z, core),
        )

    def c_copy(i, e, source, chip):
        return remote(
            c_out.at[i, chip], c_in.at[i, source], c_send.at[i, e - 1], c_recv.at[i, e - 1],
            at(x, chip, core),
        )

    def p_copy(i, d, f, run, group, half):
        there = pl.ds(i * few, few)
        return remote(
            p_out.at[run, there], p_in.at[group * 2 + half, there],
            p_send.at[i, nth(d, f)], p_recv.at[i, nth(d, f)], column_peer(d, f),
        )

    def p_sent(i, d, f):
        return p_copy(i, d, f, core_at(f) * ny + lax.rem(y + d, ny), y, core)

    def p_got(i, d, f):
        return p_copy(i, d, f, core * ny + y, lax.rem(y + ny - d, ny), core_at(f))

    def lanes_of(first, j):
        return pl.ds(pl.multiple_of((first + j) * DH, DH), DH)

    z_order = [e for e in (2, 1, 3) if e < nz]

    def make_states(i, send=False):
        for d, f in column + [(0, 0)]:
            begin = pl.multiple_of(
                (lax.rem(y + d, ny) * 2 + core_at(f)) * per_owner, per_owner
            )
            decays = dec_row[pl.ds(begin, per_owner), :]
            for j in range(i * few, (i + 1) * few):
                lanes = lanes_of(begin, j)
                decayed = (k[:, lanes].T.astype(F32) * decays[j : j + 1]).astype(BF16)
                state = jnp.dot(decayed, v[:, lanes], preferred_element_type=F32).astype(BF16)
                if (d, f) == (0, 0):
                    s_in[core * ny + y, j] = state
                else:
                    s_out[begin + j] = state
            if send and (d, f) != (0, 0):
                s_sent(i, d, f).start()

    def send_states(i):
        for d, f in column:
            s_sent(i, d, f).start()

    causal = lax.broadcasted_iota(jnp.int32, (rows, rows), 0) >= lax.broadcasted_iota(
        jnp.int32, (rows, rows), 1
    )
    def make_inside(first, count):
        for head in range(first, first + count):
            lanes = slice(head * DH, (head + 1) * DH)
            scores = lax.dot_general(
                q[:, lanes], k[:, lanes], (((1,), (1,)), ((), ())), preferred_element_type=F32
            )
            gap = cum_col[:, head : head + 1] - cum_row[head : head + 1, :]
            weights = (scores * jnp.exp(jnp.where(causal, gap, -jnp.inf))).astype(BF16)
            inside[:, lanes] = jnp.dot(weights, v[:, lanes], preferred_element_type=F32)
            gated[:, lanes] = jax.nn.sigmoid(g[:, lanes].astype(F32)) * gain[head : head + 1, :]

    def await_states(i):
        for d, f in column:
            s_got(i, d, f).wait_recv()

    def make_totals(i):
        for j in range(few):
            local = i * few + j
            total = s_in[0, local].astype(F32)
            for run in range(1, runs):
                total = total * run_decay[run, local : local + 1, :] + s_in[run, local].astype(F32)
            for n in range(pieces):
                b_out[i, j * pieces + n, :piece, :] = total[n * piece : (n + 1) * piece]
                b_out[i, j * pieces + n, piece:, :] = jnp.broadcast_to(
                    all_decay[local : local + 1, :], (PAD, DH)
                )
        for e in z_order:
            b_copy(i, e, z, lax.rem(z + e, nz)).start()
        b_in[i, z] = b_out[i, z]

    def make_group_total(i):
        for e in range(1, nz):
            b_copy(i, e, lax.rem(z + nz - e, nz), lax.rem(z + e, nz)).wait_recv()
        total = b_in[i, 0, :piece, :]
        decay = b_in[i, 0, piece:, :]
        for chip in range(1, nz):
            step = b_in[i, chip, piece:, :]
            total = total * step[:1] + b_in[i, chip, :piece, :]
            decay = decay * step
        t_out[i, :piece, :] = total
        t_out[i, piece:, :] = decay
        for d in range(1, nx):

            @pl.when(x + d < nx)
            def _(d=d):
                t_copy(i, d).start()

    def make_carried(i):
        c_now[...] = jnp.zeros_like(c_now)
        for d in range(nx - 1, 0, -1):

            @pl.when(x >= d)
            def _(d=d):
                t_copy(i, d).wait_recv()
                c_now[...] = c_now[...] * t_in[i, d - 1, piece : piece + 1, :] + t_in[i, d - 1, :piece, :]

        state = c_now[...]
        for chip in range(nz):
            c_out[i, chip] = state
            if chip + 1 < nz:
                state = state * b_in[i, chip, piece : piece + 1, :] + b_in[i, chip, :piece, :]
        for e in z_order:
            c_copy(i, e, z, lax.rem(z + e, nz)).start()
        c_in[i, z] = c_out[i, z]

    def make_prefixes(i):
        for e in range(1, nz):
            c_copy(i, e, lax.rem(z + nz - e, nz), lax.rem(z + e, nz)).wait_recv()
        for j in range(few):
            local = i * few + j
            state = c_in[i, j * pieces : (j + 1) * pieces].reshape(DH, DH)
            for run in range(runs):
                p_out[run, local] = state.astype(BF16)
                if run + 1 < runs:
                    decay = run_decay[run, local : local + 1, :]
                    state = state * decay + s_in[run, local].astype(F32)
        for d, f in column:
            p_sent(i, d, f).start()
        there = pl.ds(i * few, few)
        p_in[y * 2 + core, there] = p_out[core * ny + y, there]

    def make_outputs(i, d):
        group = lax.rem(y + ny - d, ny)
        for f in (0, 1):
            if (d, f) in column:
                p_got(i, d, f).wait_recv()
        for half in (0, 1):
            first = (group * 2 + half) * per_owner + i * few
            columns = pltpu.roll(exp_col[...], lax.rem(DH - first, DH), axis=1)[:, :few]
            for j in range(few):
                lanes = lanes_of(first, j)
                from_state = jnp.dot(
                    q[:, lanes], p_in[group * 2 + half, i * few + j], preferred_element_type=F32
                )
                mixed = inside[:, lanes] + columns[:, j : j + 1] * from_state
                scale = lax.rsqrt(jnp.mean(mixed * mixed, axis=1, keepdims=True) + 1e-6)
                o[:, lanes] = (mixed * scale * gated[:, lanes]).astype(BF16)

    def ready_rest():
        loads[4].wait()
        loads[5].wait()
        for d in range(1, ny):
            gain_copy(d, lax.rem(y + ny - d, ny)).wait_recv()
        for group in range(ny):
            gain[pl.ds(group * 2 * per_owner, 2 * per_owner), :] = gain_in[group].astype(F32)
        make_columns()
        make_decays()

    def drain_first(_):
        for d in range(1, ny):
            ld_copy(d, y, lax.rem(y + d, ny)).wait_send()
            gain_copy(d, y).wait_send()
        other_copy(1 - core, core).wait_send()

    def drain_up(i):
        for d, f in column:
            s_sent(i, d, f).wait_send()
        for e in range(1, nz):
            b_copy(i, e, z, lax.rem(z + e, nz)).wait_send()

    def drain_middle(i):
        for e in range(1, nz):
            c_copy(i, e, z, lax.rem(z + e, nz)).wait_send()
        for d in range(1, nx):

            @pl.when(x + d < nx)
            def _(d=d):
                t_copy(i, d).wait_send()

    def drain_down(i):
        for d, f in column:
            p_sent(i, d, f).wait_send()

    sixteenth = heads // 16
    plan = " ".join(SCHEDULE).split()
    inner = iter(range(16))
    calls = dict(
        S=make_states, s=send_states, F=functools.partial(make_states, send=True), W=await_states, T=make_totals,
        G=make_group_total, K=make_carried, X=make_prefixes,
        A=drain_first, U=drain_up, M=drain_middle, P=drain_down,
    )
    for word in plan:
        if word == "r":
            ready_rest()
        elif word == "I":
            make_inside(next(inner) * sixteenth, sixteenth)
        elif word[0] == "O":
            make_outputs(int(word[1]), int(word[2]))
        else:
            calls[word[0]](int(word[1]))


def on_device(dims, queries, keys, values, gate, log_decay, norm_gain):
    ny, nx, nz, chunks, few = dims
    per_owner = chunks * few
    piece = DH * few // nz
    runs = 2 * ny
    heads = runs * per_owner
    _, rows, width = queries.shape
    block = log_decay.shape[2]
    dma = pltpu.SemaphoreType.DMA
    vmem = pltpu.VMEM
    stream = [vmem((rows, width), BF16)] * 4
    out = pl.pallas_call(
        functools.partial(kernel, dims),
        out_shape=pltpu.VMEM((rows, width), BF16),
        in_specs=[pl.BlockSpec(memory_space=pltpu.HBM)] * 6,
        out_specs=pl.BlockSpec(memory_space=pltpu.VMEM),
        scratch_shapes=stream
        + [
            vmem((2 * per_owner, block), F32),
            vmem((ny, 2 * per_owner, rows), F32),
            vmem((2, per_owner, block), F32),
            vmem((ny, 2 * per_owner, DH), BF16),
            vmem((heads, DH), F32),
            vmem((heads, rows), F32),
            vmem((heads, rows), F32),
            vmem((rows, rows), F32),
            vmem((rows, rows), F32),
            vmem((runs, per_owner, DH), F32),
            vmem((per_owner, DH), F32),
            vmem((heads, DH, DH), BF16),
            vmem((runs, per_owner, DH, DH), BF16),
            vmem((chunks, nz, piece + PAD, DH), F32),
            vmem((chunks, nz, piece + PAD, DH), F32),
            vmem((chunks, piece + PAD, DH), F32),
            vmem((chunks, nx - 1, piece + PAD, DH), F32),
            vmem((piece, DH), F32),
            vmem((chunks, nz, piece, DH), F32),
            vmem((chunks, nz, piece, DH), F32),
            vmem((runs, per_owner, DH, DH), BF16),
            vmem((runs, per_owner, DH, DH), BF16),
            vmem((rows, width), F32),
            vmem((rows, width), F32),
            dma((6,)),
            dma((ny - 1,)),
            dma((ny - 1,)),
            dma((1,)),
            dma((1,)),
            dma((ny - 1,)),
            dma((ny - 1,)),
            dma((chunks, runs - 1)),
            dma((chunks, runs - 1)),
            dma((chunks, nz - 1)),
            dma((chunks, nz - 1)),
            dma((chunks, nx - 1)),
            dma((chunks, nx - 1)),
            dma((chunks, nz - 1)),
            dma((chunks, nz - 1)),
            dma((chunks, runs - 1)),
            dma((chunks, runs - 1)),
        ],
        compiler_params=pltpu.CompilerParams(
            collective_id=0, has_side_effects=True, vmem_limit_bytes=52 * 2**20
        ),
        cost_estimate=pl.CostEstimate(
            flops=8 * rows * DH * width, bytes_accessed=10 * rows * width, transcendentals=0
        ),
    )(
        queries[0],
        keys[0],
        values[0],
        gate[0],
        log_decay[0],
        norm_gain.reshape(2 * per_owner, DH),
    )
    return out[None]


def solution(mesh):
    ny = mesh.shape["head"]
    nctx = mesh.shape["ctx"]
    nx = 4 if nctx >= 16 else 2
    def whole(queries, keys, values, gate, log_decay, norm_gain):
        chunks = CHUNKS
        few = log_decay.shape[1] // (2 * ny * chunks)
        dims = (ny, nx, nctx // (2 * nx), chunks, few)
        return jax.shard_map(
            functools.partial(on_device, dims),
            mesh=mesh,
            in_specs=(P("ctx", "head", None),) * 5 + (P("head"),),
            out_specs=P("ctx", "head", None),
            check_vma=False,
        )(queries, keys, values, gate, log_decay, norm_gain)

    return whole
```

```python
import functools

import jax
import jax.numpy as jnp
from jax import lax
from jax.experimental import pallas as pl
from jax.experimental.pallas import tpu as pltpu
from jax.sharding import PartitionSpec as P

MESH = pl.DeviceIdType.MESH
F32 = jnp.float32
BF16 = jnp.bfloat16
DH = 128
CHUNKS = 4
SCHEDULE = (
    "F0 S1 r I",
    "s1 S2 S3 I",
    "I I I A0",
    "W0 s2 T0 I",
    "I W1 s3 T1",
    "G0 I I K0",
    "I G1 I X0",
    "W2 T2 K1 I",
    "I G2 X1 I",
    "W3 T3 K2 I",
    "G3 X2 I K3",
    "U0 U1 O00 O02",
    "O01 O03 X3 U2",
    "M0 M1 O10 O12",
    "O11 O13 P0 U3",
    "M2 M3 O20 O22",
    "O21 O23 P1 P2",
    "O30 O32 O31 O33",
    "P3",
)
PAD = 8
HIGHEST = lax.Precision.HIGHEST


def kernel(
    dims,
    q_hbm, k_hbm, v_hbm, g_hbm, ld_hbm, gain_hbm,
    o,
    q, k, v, g,
    ld, ld_mine, run_ld, gain_in, gain,
    cum_row, dec_row, cum_col, exp_col, run_decay, all_decay,
    s_out, s_in, b_out, b_in, t_out, t_in, c_now, c_out, c_in, p_out, p_in,
    inside, gated,
    load_sem,
    ld_send, ld_recv, other_send, other_recv, gain_send, gain_recv,
    s_send, s_recv, b_send, b_recv, t_send, t_recv, c_send, c_recv, p_send, p_recv,
):
    ny, nx, nz, chunks, few = dims
    rows = q.shape[0]
    per_owner = chunks * few
    heads = 2 * ny * per_owner
    pieces = nz // few
    runs = 2 * ny
    piece = DH // pieces
    y = lax.axis_index("head")
    ctx = lax.axis_index("ctx")
    x = ctx // (2 * nz)
    z = (ctx // 2) % nz
    core = ctx % 2

    def at(x, z, core):
        return {"ctx": (x * nz + z) * 2 + core}

    def load(n, src, dst):
        return pltpu.make_async_copy(src, dst, load_sem.at[n])

    loads = [
        load(0, ld_hbm, ld),
        load(1, gain_hbm, gain_in.at[y]),
        load(2, k_hbm, k),
        load(3, v_hbm, v),
        load(4, q_hbm, q),
        load(5, g_hbm, g),
    ]
    for one in loads:
        one.start()

    barrier = pltpu.get_barrier_semaphore()
    column = [(d, f) for d in (2, 1, 3, 0) for f in (0, 1) if d < ny and (d, f) != (0, 0)]

    def core_at(f):
        return 1 - core if f else core

    def column_peer(d, f):
        return {"head": lax.rem(y + d, ny), **at(x, z, core_at(f))}

    def nth(d, f):
        return 2 * d + f - 1

    peers = [column_peer(d, f) for d, f in column]
    peers += [at(x, lax.rem(z + e, nz), core) for e in range(1, nz)]
    for peer in peers:
        pl.semaphore_signal(barrier, inc=1, device_id=peer, device_id_type=MESH)
    for d in range(1, nx):

        @pl.when(x >= d)
        def _(d=d):
            pl.semaphore_signal(
                barrier, inc=1, device_id=at(x - d, z, core), device_id_type=MESH
            )

    pl.semaphore_wait(barrier, len(peers) + nx - 1 - x)

    def remote(src, dst, send, recv, peer):
        return pltpu.make_async_remote_copy(
            src_ref=src, dst_ref=dst, send_sem=send, recv_sem=recv,
            device_id=peer, device_id_type=MESH,
        )

    def ld_copy(d, source, reader):
        theirs = pl.ds(pl.multiple_of(reader * rows, rows), rows)
        return remote(
            ld.at[:, theirs], ld_mine.at[source], ld_send.at[d - 1], ld_recv.at[d - 1],
            {"head": lax.rem(y + d, ny)},
        )

    def gain_copy(d, source):
        peer = {"head": lax.rem(y + d, ny)}
        return remote(
            gain_in.at[source], gain_in.at[source], gain_send.at[d - 1], gain_recv.at[d - 1], peer
        )

    def other_copy(half, block):
        rows_of = pl.ds(pl.multiple_of(half * per_owner, per_owner), per_owner)
        return remote(
            ld.at[rows_of], run_ld.at[block], other_send.at[0], other_recv.at[0], column_peer(0, 1)
        )

    loads[0].wait()
    for d in [d for d in (2, 1, 3) if d < ny]:
        ld_copy(d, y, lax.rem(y + d, ny)).start()
    mine = pl.ds(pl.multiple_of(y * rows, rows), rows)
    other_copy(1 - core, core).start()
    loads[1].wait()
    for d in range(1, ny):
        gain_copy(d, y).start()
    ld_mine[y] = ld[:, mine]
    run_ld[core] = ld[pl.ds(pl.multiple_of(core * per_owner, per_owner), per_owner), :]
    upper = (
        lax.broadcasted_iota(jnp.int32, (rows, rows), 0)
        <= lax.broadcasted_iota(jnp.int32, (rows, rows), 1)
    ).astype(F32)
    loads[2].wait()
    loads[3].wait()
    for d in range(1, ny):
        ld_copy(d, lax.rem(y + ny - d, ny), y).wait_recv()

    cumulative = jnp.dot(
        ld_mine[...].reshape(heads, rows), upper, precision=HIGHEST, preferred_element_type=F32
    )
    dec_row[...] = jnp.exp(cumulative[:, rows - 1 :] - cumulative)
    cum_row[...] = cumulative

    def make_columns():
        cum_col[:heads, :] = cum_row[...]
        if heads < rows:
            cum_col[heads:, :] = jnp.zeros((rows - heads, rows), F32)
        cum_col[...] = cum_col[...].T
        exp_col[...] = jnp.exp(cum_col[...])

    def make_decays():
        other_copy(core, 1 - core).wait_recv()
        whole = jnp.zeros((per_owner, 1), F32)
        for run in range(runs):
            part = run_ld[run // ny, :, run % ny * rows : (run % ny + 1) * rows]
            total = jnp.sum(part, axis=1, keepdims=True)
            run_decay[run] = jnp.broadcast_to(jnp.exp(total), (per_owner, DH))
            whole = whole + total
        all_decay[...] = jnp.broadcast_to(jnp.exp(whole), (per_owner, DH))

    def s_copy(i, d, f, source, group, half):
        first = (group * 2 + half) * per_owner + i * few
        there = pl.ds(i * few, few)
        return remote(
            s_out.at[pl.ds(first, few)], s_in.at[source, there],
            s_send.at[i, nth(d, f)], s_recv.at[i, nth(d, f)], column_peer(d, f),
        )

    def s_sent(i, d, f):
        return s_copy(i, d, f, core * ny + y, lax.rem(y + d, ny), core_at(f))

    def s_got(i, d, f):
        return s_copy(i, d, f, core_at(f) * ny + lax.rem(y + ny - d, ny), y, core)

    def b_copy(i, e, source, owner):
        return remote(
            b_out.at[i, owner], b_in.at[i, source], b_send.at[i, e - 1], b_recv.at[i, e - 1],
            at(x, owner, core),
        )

    def t_copy(i, d):
        return remote(
            t_out.at[i], t_in.at[i, d - 1], t_send.at[i, d - 1], t_recv.at[i, d - 1],
            at(lax.rem(x + d, nx), z, core),
        )

    def c_copy(i, e, source, chip):
        return remote(
            c_out.at[i, chip], c_in.at[i, source], c_send.at[i, e - 1], c_recv.at[i, e - 1],
            at(x, chip, core),
        )

    def p_copy(i, d, f, run, group, half):
        there = pl.ds(i * few, few)
        return remote(
            p_out.at[run, there], p_in.at[group * 2 + half, there],
            p_send.at[i, nth(d, f)], p_recv.at[i, nth(d, f)], column_peer(d, f),
        )

    def p_sent(i, d, f):
        return p_copy(i, d, f, core_at(f) * ny + lax.rem(y + d, ny), y, core)

    def p_got(i, d, f):
        return p_copy(i, d, f, core * ny + y, lax.rem(y + ny - d, ny), core_at(f))

    def lanes_of(first, j):
        return pl.ds(pl.multiple_of((first + j) * DH, DH), DH)

    z_order = [e for e in (2, 1, 3) if e < nz]

    def make_states(i, send=False):
        for d, f in column + [(0, 0)]:
            begin = pl.multiple_of(
                (lax.rem(y + d, ny) * 2 + core_at(f)) * per_owner, per_owner
            )
            decays = dec_row[pl.ds(begin, per_owner), :]
            for j in range(i * few, (i + 1) * few):
                lanes = lanes_of(begin, j)
                decayed = (k[:, lanes].T.astype(F32) * decays[j : j + 1]).astype(BF16)
                state = jnp.dot(decayed, v[:, lanes], preferred_element_type=F32).astype(BF16)
                if (d, f) == (0, 0):
                    s_in[core * ny + y, j] = state
                else:
                    s_out[begin + j] = state
            if send and (d, f) != (0, 0):
                s_sent(i, d, f).start()

    def send_states(i):
        for d, f in column:
            s_sent(i, d, f).start()

    causal = lax.broadcasted_iota(jnp.int32, (rows, rows), 0) >= lax.broadcasted_iota(
        jnp.int32, (rows, rows), 1
    )
    def make_inside(first, count):
        for head in range(first, first + count):
            lanes = slice(head * DH, (head + 1) * DH)
            scores = lax.dot_general(
                q[:, lanes], k[:, lanes], (((1,), (1,)), ((), ())), preferred_element_type=F32
            )
            gap = cum_col[:, head : head + 1] - cum_row[head : head + 1, :]
            weights = (scores * jnp.exp(jnp.where(causal, gap, -jnp.inf))).astype(BF16)
            inside[:, lanes] = jnp.dot(weights, v[:, lanes], preferred_element_type=F32)
            gated[:, lanes] = jax.nn.sigmoid(g[:, lanes].astype(F32)) * gain[head : head + 1, :]

    def await_states(i):
        for d, f in column:
            s_got(i, d, f).wait_recv()

    def make_totals(i):
        for j in range(few):
            local = i * few + j
            total = s_in[0, local].astype(F32)
            for run in range(1, runs):
                total = total * run_decay[run, local : local + 1, :] + s_in[run, local].astype(F32)
            for n in range(pieces):
                b_out[i, j * pieces + n, :piece, :] = total[n * piece : (n + 1) * piece]
                b_out[i, j * pieces + n, piece:, :] = jnp.broadcast_to(
                    all_decay[local : local + 1, :], (PAD, DH)
                )
        for e in z_order:
            b_copy(i, e, z, lax.rem(z + e, nz)).start()
        b_in[i, z] = b_out[i, z]

    def make_group_total(i):
        for e in range(1, nz):
            b_copy(i, e, lax.rem(z + nz - e, nz), lax.rem(z + e, nz)).wait_recv()
        total = b_in[i, 0, :piece, :]
        decay = b_in[i, 0, piece:, :]
        for chip in range(1, nz):
            step = b_in[i, chip, piece:, :]
            total = total * step[:1] + b_in[i, chip, :piece, :]
            decay = decay * step
        t_out[i, :piece, :] = total
        t_out[i, piece:, :] = decay
        for d in range(1, nx):

            @pl.when(x + d < nx)
            def _(d=d):
                t_copy(i, d).start()

    def make_carried(i):
        c_now[...] = jnp.zeros_like(c_now)
        for d in range(nx - 1, 0, -1):

            @pl.when(x >= d)
            def _(d=d):
                t_copy(i, d).wait_recv()
                c_now[...] = c_now[...] * t_in[i, d - 1, piece : piece + 1, :] + t_in[i, d - 1, :piece, :]

        state = c_now[...]
        for chip in range(nz):
            c_out[i, chip] = state
            if chip + 1 < nz:
                state = state * b_in[i, chip, piece : piece + 1, :] + b_in[i, chip, :piece, :]
        for e in z_order:
            c_copy(i, e, z, lax.rem(z + e, nz)).start()
        c_in[i, z] = c_out[i, z]

    def make_prefixes(i):
        for e in range(1, nz):
            c_copy(i, e, lax.rem(z + nz - e, nz), lax.rem(z + e, nz)).wait_recv()
        for j in range(few):
            local = i * few + j
            state = c_in[i, j * pieces : (j + 1) * pieces].reshape(DH, DH)
            for run in range(runs):
                p_out[run, local] = state.astype(BF16)
                if run + 1 < runs:
                    decay = run_decay[run, local : local + 1, :]
                    state = state * decay + s_in[run, local].astype(F32)
        for d, f in column:
            p_sent(i, d, f).start()
        there = pl.ds(i * few, few)
        p_in[y * 2 + core, there] = p_out[core * ny + y, there]

    def make_outputs(i, d):
        group = lax.rem(y + ny - d, ny)
        for f in (0, 1):
            if (d, f) in column:
                p_got(i, d, f).wait_recv()
        for half in (0, 1):
            first = (group * 2 + half) * per_owner + i * few
            columns = pltpu.roll(exp_col[...], lax.rem(DH - first, DH), axis=1)[:, :few]
            for j in range(few):
                lanes = lanes_of(first, j)
                from_state = jnp.dot(
                    q[:, lanes], p_in[group * 2 + half, i * few + j], preferred_element_type=F32
                )
                mixed = inside[:, lanes] + columns[:, j : j + 1] * from_state
                scale = lax.rsqrt(jnp.mean(mixed * mixed, axis=1, keepdims=True) + 1e-6)
                o[:, lanes] = (mixed * scale * gated[:, lanes]).astype(BF16)

    def ready_rest():
        loads[4].wait()
        loads[5].wait()
        for d in range(1, ny):
            gain_copy(d, lax.rem(y + ny - d, ny)).wait_recv()
        for group in range(ny):
            gain[pl.ds(group * 2 * per_owner, 2 * per_owner), :] = gain_in[group].astype(F32)
        make_columns()
        make_decays()

    def drain_first(_):
        for d in range(1, ny):
            ld_copy(d, y, lax.rem(y + d, ny)).wait_send()
            gain_copy(d, y).wait_send()
        other_copy(1 - core, core).wait_send()

    def drain_up(i):
        for d, f in column:
            s_sent(i, d, f).wait_send()
        for e in range(1, nz):
            b_copy(i, e, z, lax.rem(z + e, nz)).wait_send()

    def drain_middle(i):
        for e in range(1, nz):
            c_copy(i, e, z, lax.rem(z + e, nz)).wait_send()
        for d in range(1, nx):

            @pl.when(x + d < nx)
            def _(d=d):
                t_copy(i, d).wait_send()

    def drain_down(i):
        for d, f in column:
            p_sent(i, d, f).wait_send()

    sixteenth = heads // 16
    plan = " ".join(SCHEDULE).split()
    inner = iter(range(16))
    calls = dict(
        S=make_states, s=send_states, F=functools.partial(make_states, send=True), W=await_states, T=make_totals,
        G=make_group_total, K=make_carried, X=make_prefixes,
        A=drain_first, U=drain_up, M=drain_middle, P=drain_down,
    )
    for word in plan:
        if word == "r":
            ready_rest()
        elif word == "I":
            make_inside(next(inner) * sixteenth, sixteenth)
        elif word[0] == "O":
            make_outputs(int(word[1]), int(word[2]))
        else:
            calls[word[0]](int(word[1]))


def on_device(dims, queries, keys, values, gate, log_decay, norm_gain):
    ny, nx, nz, chunks, few = dims
    per_owner = chunks * few
    piece = DH * few // nz
    runs = 2 * ny
    heads = runs * per_owner
    _, rows, width = queries.shape
    block = log_decay.shape[2]
    dma = pltpu.SemaphoreType.DMA
    vmem = pltpu.VMEM
    stream = [vmem((rows, width), BF16)] * 4
    out = pl.pallas_call(
        functools.partial(kernel, dims),
        out_shape=pltpu.VMEM((rows, width), BF16),
        in_specs=[pl.BlockSpec(memory_space=pltpu.HBM)] * 6,
        out_specs=pl.BlockSpec(memory_space=pltpu.VMEM),
        scratch_shapes=stream
        + [
            vmem((2 * per_owner, block), F32),
            vmem((ny, 2 * per_owner, rows), F32),
            vmem((2, per_owner, block), F32),
            vmem((ny, 2 * per_owner, DH), BF16),
            vmem((heads, DH), F32),
            vmem((heads, rows), F32),
            vmem((heads, rows), F32),
            vmem((rows, rows), F32),
            vmem((rows, rows), F32),
            vmem((runs, per_owner, DH), F32),
            vmem((per_owner, DH), F32),
            vmem((heads, DH, DH), BF16),
            vmem((runs, per_owner, DH, DH), BF16),
            vmem((chunks, nz, piece + PAD, DH), F32),
            vmem((chunks, nz, piece + PAD, DH), F32),
            vmem((chunks, piece + PAD, DH), F32),
            vmem((chunks, nx - 1, piece + PAD, DH), F32),
            vmem((piece, DH), F32),
            vmem((chunks, nz, piece, DH), F32),
            vmem((chunks, nz, piece, DH), F32),
            vmem((runs, per_owner, DH, DH), BF16),
            vmem((runs, per_owner, DH, DH), BF16),
            vmem((rows, width), F32),
            vmem((rows, width), F32),
            dma((6,)),
            dma((ny - 1,)),
            dma((ny - 1,)),
            dma((1,)),
            dma((1,)),
            dma((ny - 1,)),
            dma((ny - 1,)),
            dma((chunks, runs - 1)),
            dma((chunks, runs - 1)),
            dma((chunks, nz - 1)),
            dma((chunks, nz - 1)),
            dma((chunks, nx - 1)),
            dma((chunks, nx - 1)),
            dma((chunks, nz - 1)),
            dma((chunks, nz - 1)),
            dma((chunks, runs - 1)),
            dma((chunks, runs - 1)),
        ],
        compiler_params=pltpu.CompilerParams(
            collective_id=0, has_side_effects=True, vmem_limit_bytes=52 * 2**20
        ),
        cost_estimate=pl.CostEstimate(
            flops=8 * rows * DH * width, bytes_accessed=10 * rows * width, transcendentals=0
        ),
    )(
        queries[0],
        keys[0],
        values[0],
        gate[0],
        log_decay[0],
        norm_gain.reshape(2 * per_owner, DH),
    )
    return out[None]


def solution(mesh):
    ny = mesh.shape["head"]
    nctx = mesh.shape["ctx"]
    nx = 4 if nctx >= 16 else 2
    def whole(queries, keys, values, gate, log_decay, norm_gain):
        chunks = CHUNKS
        few = log_decay.shape[1] // (2 * ny * chunks)
        dims = (ny, nx, nctx // (2 * nx), chunks, few)
        return jax.shard_map(
            functools.partial(on_device, dims),
            mesh=mesh,
            in_specs=(P("ctx", "head", None),) * 5 + (P("head"),),
            out_specs=P("ctx", "head", None),
            check_vma=False,
        )(queries, keys, values, gate, log_decay, norm_gain)

    return whole
```
